32 devices in a mesh: seq: 8 (over z, x), inner: 4 (over y, core).
Axes of the slice: x: 2, y: 2, z: 4, core: 2. Of those that a mesh axis runs over, the one named last changes fastest.
Arguments:
- log_mel: bfloat16 [28672, 320], P(('seq', 'inner')), may hold values from -6 to 6
- lengths: int32 [32, 4], replicated, may hold values from 1 to 893, as said below
- first_kernel: bfloat16 [9, 128], replicated, may hold values from -2 to 2
- first_bias: float32 [128], replicated, may hold values from -3 to 3
- second_kernel: bfloat16 [1152, 128], replicated, may hold values from -0.1875 to 0.1875
- second_bias: float32 [128], replicated, may hold values from -3 to 3
- embed_weight: bfloat16 [2560, 1024], replicated, may hold values from -0.125 to 0.125
- norm_gain: float32 [1024], replicated, may hold values from 0.1 to 1.9
- head_weight: bfloat16 [1024, 3072], replicated
- output_weight: bfloat16 [1024, 1024], replicated, may hold values from -0.1875 to 0.1875
Outputs:
- encoded: bfloat16 [16384, 1024], P(('seq', 'inner'))
The draws below stay inside these ranges and needn't reach their ends.
Inputs may be any that keep to these rules, and one draw needn't show every extreme that they name: `lengths`: every length is 1 or more. The frames of owner d begin at d * 512 + e_d with e_d between -192 and 192; e_0 = 0, the frames of all owners together are exactly 16384, and in every draw some owner has e_d = 192 and another e_d = -192. In every draw some utterance has exactly 893 frames.
All inputs are finite; a program needn't handle non-finite values.
Results may differ from the reference program's by a relative error of at most 0.008.
The reference program's roundings to bfloat16 on the way count: a program that leaves them out, or rounds other values in their place, can miss the bound.
Values may be sent and summed in bfloat16 or wider, within the bound.
No kernel may reach another device: no remote copies, remote signals or barrier semaphores. Data moves between devices by JAX's collectives and lax.ppermute only.
A program may use at most 256 MiB of HBM per device.

```python
import jax
import jax.numpy as jnp
from jax import lax

MEL = 80
CH = 128
D = 1024
HEADS = 16
SPAN = 64
LEFT_SPANS = 4
CTX = 320
SHARD = 512
MARGIN = 192
CAP = 896
UTT_DEV = 4
FRAMES = 16384
DEVICES = 32


def draw_lengths(key, part):
    key_drift, key_pick, key_share = jax.random.split(jax.random.fold_in(key, 11), 3)
    owners = DEVICES
    drift = jax.random.randint(key_drift, (owners + 1,), -MARGIN, MARGIN + 1)
    picked = jax.random.randint(key_pick, (), 1, owners - 1)
    places = jnp.arange(owners + 1)
    drift = jnp.where(places == picked, -MARGIN, drift)
    drift = jnp.where(places == picked + 1, MARGIN, drift)
    drift = jnp.where((places == 0) | (places == owners), 0, drift)
    counts = SHARD + drift[1:] - drift[:-1]
    shares = jax.random.randint(key_share, (owners, UTT_DEV), 1, 5)
    totals = jnp.sum(shares, axis=1, keepdims=True)
    edges = counts[:, None] * jnp.cumsum(shares, axis=1) // totals
    lower_edges = jnp.concatenate([jnp.zeros((owners, 1), edges.dtype), edges[:, :-1]], axis=1)
    split = edges - lower_edges
    columns = jnp.arange(UTT_DEV)
    forced = jnp.where(columns == UTT_DEV - 1, CAP - UTT_DEV + 1, 1)
    rows = jnp.arange(owners)
    result = jnp.where((rows == picked)[:, None], forced[None, :], split)
    return result.astype(jnp.int32)


def draw_head_weight(key, part):
    key_base = jax.random.fold_in(jax.random.fold_in(key, 7), 0)
    return (jax.random.normal(key_base, (D, 3 * D), jnp.float32) * D ** (-0.5)).astype(jnp.bfloat16)


def block_levels(own_key, shape, cuts, low, top_value):
    def one(dim, shards_of):
        draws = jax.random.uniform(jax.random.fold_in(jax.random.fold_in(own_key, 6), dim), (shards_of,), jnp.float32, low / len(cuts), top_value / len(cuts))
        return jnp.repeat(jnp.exp(draws), shape[dim] // shards_of).reshape((-1,) + (1,) * (len(shape) - dim - 1))

    level = one(*cuts[0])
    for cut in cuts[1:]:
        level = level * one(*cut)
    return level


def noise(own_key, dims, scale, bound, shards=(), held_as=jnp.bfloat16):
    values = scale * jax.random.normal(own_key, dims, jnp.float32)
    if shards:
        values = values * block_levels(own_key, dims, shards, -0.22, 0.18)
    return jnp.clip(values, -bound, bound).astype(held_as)


def setup_inputs(seed: int = 0) -> dict:
    arg_keys = jax.random.split(jax.random.key(seed), 11)
    log_mel = noise(arg_keys[0], (DEVICES * CAP, 4 * MEL), 1.0, 6.0, ((0, 32),))
    lengths = draw_lengths(jax.random.fold_in(arg_keys[10], 71), 0)
    first_kernel = noise(arg_keys[2], (9, CH), 9 ** -0.5, 2.0)
    first_bias = noise(arg_keys[3], (CH,), 0.5, 3.0, (), jnp.float32)
    second_kernel = noise(arg_keys[4], (9 * CH, CH), (9 * CH) ** -0.5, 0.1875)
    second_bias = noise(arg_keys[5], (CH,), 0.5, 3.0, (), jnp.float32)
    embed_weight = noise(arg_keys[6], ((MEL // 4) * CH, D), ((MEL // 4) * CH) ** -0.5, 0.125)
    norm_gain = jnp.clip(1.0 + 0.18 * jax.random.normal(arg_keys[7], (D,), jnp.float32), 0.1, 1.9)
    head_weight = draw_head_weight(jax.random.fold_in(arg_keys[10], 71), 0)
    output_weight = noise(arg_keys[9], (D, D), D ** -0.5, 0.1875)
    return dict(log_mel=log_mel, lengths=lengths, first_kernel=first_kernel, first_bias=first_bias, second_kernel=second_kernel, second_bias=second_bias, embed_weight=embed_weight, norm_gain=norm_gain, head_weight=head_weight, output_weight=output_weight)


def front_end(raw_rows, seg_ids, first_kernel, first_bias, second_kernel, second_bias, embed_weight):
    row_count = raw_rows.shape[0] - 1
    mel_bins = raw_rows.shape[1] // 4
    usable = seg_ids >= 0
    joined = jnp.concatenate([jnp.zeros((1,), bool), (seg_ids[1:] == seg_ids[:-1]) & usable[1:]])
    frames = jnp.where(usable[:, None], raw_rows, jnp.zeros_like(raw_rows)).reshape(row_count + 1, 4, mel_bins)
    shifted = jnp.concatenate([jnp.zeros((1, mel_bins), raw_rows.dtype), frames[:-1, 3]], axis=0)
    before = jnp.where(joined[:, None], shifted, jnp.zeros_like(shifted))
    even_taps = jnp.stack([before, frames[:, 0], frames[:, 1]], axis=1)
    odd_taps = jnp.stack([frames[:, 1], frames[:, 2], frames[:, 3]], axis=1)
    time_taps = jnp.stack([even_taps, odd_taps], axis=1)
    padded = jnp.pad(time_taps, ((0, 0), (0, 0), (0, 0), (1, 0)))
    freq_taps = jnp.stack([padded[..., 0:mel_bins:2], padded[..., 1:mel_bins + 1:2], padded[..., 2:mel_bins + 2:2]], axis=-1)
    patches = jnp.transpose(freq_taps, (0, 1, 3, 2, 4)).reshape(-1, 9)
    first_out = jnp.dot(patches, first_kernel, preferred_element_type=jnp.float32) + first_bias
    first_out = jnp.maximum(first_out, 0.0).astype(jnp.bfloat16).reshape(row_count + 1, 2, mel_bins // 2, -1)
    channels = first_out.shape[-1]
    earlier = jnp.where(joined[1:, None, None], first_out[:-1, 1], jnp.zeros_like(first_out[:-1, 1]))
    second_in = jnp.stack([earlier, first_out[1:, 0], first_out[1:, 1]], axis=1)
    half_bins = mel_bins // 2
    spread = jnp.pad(second_in, ((0, 0), (0, 0), (1, 0), (0, 0)))
    summed = jnp.zeros((row_count * (half_bins // 2), second_kernel.shape[1]), jnp.float32)
    for tap_time in range(3):
        for tap_freq in range(3):
            slab_rows = spread[:, tap_time, tap_freq:tap_freq + half_bins:2].reshape(-1, channels)
            offset = (tap_time * 3 + tap_freq) * channels
            summed = summed + jnp.dot(slab_rows, second_kernel[offset:offset + channels], preferred_element_type=jnp.float32)
    second_out = jnp.maximum(summed + second_bias, 0.0).astype(jnp.bfloat16).reshape(row_count, -1)
    return jnp.dot(second_out, embed_weight, preferred_element_type=jnp.float32).astype(jnp.bfloat16)

def positions(spots, starts, frame_total):
    usable = (spots >= 0) & (spots < frame_total)
    reached = starts[None, :] <= spots[:, None]
    seg_ids = lax.optimization_barrier(jnp.sum(reached.astype(jnp.int32), axis=1)).astype(jnp.int32) - 1
    begins = lax.optimization_barrier(jnp.max(jnp.where(reached, starts[None, :], jnp.zeros_like(starts[None, :])), axis=1))
    seg_ids = jnp.where(usable, seg_ids, -1).astype(jnp.int32)
    return (seg_ids, (spots - begins).astype(jnp.int32))

def visible(query_seg, query_pos, key_seg, key_pos):
    query_span = query_pos // SPAN
    key_span = key_pos // SPAN
    same_utt = (query_seg[:, None] == key_seg[None, :]) & (key_seg[None, :] >= 0)
    return same_utt & (key_span[None, :] >= query_span[:, None] - LEFT_SPANS) & (key_span[None, :] <= query_span[:, None])

def layer_norm(rows_in, gain):
    values = rows_in.astype(jnp.float32)
    center = values - lax.optimization_barrier(jnp.mean(values, axis=1, keepdims=True))
    spread = lax.optimization_barrier(jnp.mean(center * center, axis=1, keepdims=True))
    return (center * lax.rsqrt(spread + 1e-05) * gain).astype(jnp.bfloat16)

def attend(queries, keys, values, allowed):
    head_size = queries.shape[1] // HEADS
    query_heads = queries.astype(jnp.float32).reshape(-1, HEADS, head_size)
    key_heads = keys.astype(jnp.float32).reshape(-1, HEADS, head_size)
    value_heads = values.astype(jnp.float32).reshape(-1, HEADS, head_size)
    scores = jnp.einsum('qhd,khd->hqk', query_heads, key_heads) * head_size ** (-0.5)
    scores = jnp.where(allowed[None], scores, jnp.float32(-1e+30))
    peak = lax.optimization_barrier(jnp.max(scores, axis=-1, keepdims=True))
    expd = jnp.exp(scores - peak)
    probs = (expd / lax.optimization_barrier(jnp.sum(expd, axis=-1, keepdims=True))).astype(jnp.bfloat16)
    mixed = jnp.einsum('hqk,khd->qhd', probs.astype(jnp.float32), value_heads)
    return mixed.reshape(queries.shape[0], -1).astype(jnp.bfloat16)

def reference(log_mel, lengths, first_kernel, first_bias, second_kernel, second_bias, embed_weight, norm_gain, head_weight, output_weight):
    owners = lengths.shape[0]
    flat = lengths.reshape(-1).astype(jnp.int32)
    starts = (jnp.cumsum(flat) - flat).astype(jnp.int32)
    owner_len = lax.optimization_barrier(jnp.sum(lengths, axis=1)).astype(jnp.int32)
    owner_start = (jnp.cumsum(owner_len) - owner_len).astype(jnp.int32)
    spots = jnp.arange(FRAMES, dtype=jnp.int32)
    owner_of = (lax.optimization_barrier(jnp.sum((owner_start[None, :] <= spots[:, None]).astype(jnp.int32), axis=1)) - 1).astype(jnp.int32)
    source = (owner_of * CAP + spots - owner_of * SHARD + MARGIN).astype(jnp.int32)
    raw_global = jnp.take(log_mel, source, axis=0)
    raw_padded = jnp.concatenate([jnp.zeros((1, log_mel.shape[1]), log_mel.dtype), raw_global], axis=0)

    def front_block(index):
        begin = (index * SHARD).astype(jnp.int32)
        window = lax.dynamic_slice_in_dim(raw_padded, begin, SHARD + 1, 0)
        seg_ids, unused_pos = positions(begin - 1 + jnp.arange(SHARD + 1, dtype=jnp.int32), starts, FRAMES)
        return front_end(window, seg_ids, first_kernel, first_bias, second_kernel, second_bias, embed_weight)
    block_ids = jnp.arange(owners, dtype=jnp.int32)
    embedded = lax.map(front_block, block_ids).reshape(FRAMES, -1)
    normed = layer_norm(embedded, norm_gain)
    packed = jnp.dot(normed, head_weight, preferred_element_type=jnp.float32).astype(jnp.bfloat16)
    width = normed.shape[1]
    key_vals = packed[:, width:]
    kv_padded = jnp.concatenate([jnp.zeros((CTX, 2 * width), jnp.bfloat16), key_vals, jnp.zeros((SPAN, 2 * width), jnp.bfloat16)], axis=0)
    key_rows = CTX + SHARD + SPAN

    def attend_block(index):
        begin = (index * SHARD).astype(jnp.int32)
        queries = lax.dynamic_slice_in_dim(packed, begin, SHARD, 0)[:, :width]
        context = lax.dynamic_slice_in_dim(kv_padded, begin, key_rows, 0)
        query_seg, query_pos = positions(begin + jnp.arange(SHARD, dtype=jnp.int32), starts, FRAMES)
        key_seg, key_pos = positions(begin - CTX + jnp.arange(key_rows, dtype=jnp.int32), starts, FRAMES)
        allowed = visible(query_seg, query_pos, key_seg, key_pos)
        mixed = attend(queries, context[:, :width], context[:, width:], allowed)
        residual = lax.dynamic_slice_in_dim(embedded, begin, SHARD, 0)
        output = residual.astype(jnp.float32) + jnp.dot(mixed, output_weight, preferred_element_type=jnp.float32)
        return output.astype(jnp.bfloat16)
    return lax.map(attend_block, block_ids).reshape(FRAMES, -1)
```

```python
import jax
import jax.numpy as jnp
from jax import lax
from jax.experimental import pallas as pl
from jax.experimental.pallas import tpu as pltpu
from jax.sharding import PartitionSpec as P

HEADS = 16
SPAN = 64
LEFT_SPANS = 4
CTX = 320
SHARD = 512
MARGIN = 192
CAP = 896
WIN = CTX + SHARD + SPAN
MEL = 80
CH = 128
PAIRS = MEL // 4
D = 1024
HEAD = D // HEADS
ROWS = 448
QROWS = 128
KROWS = 512
AXES = ("seq", "inner")
F32 = jnp.float32
BF16 = jnp.bfloat16


def iota(shape, dim):
    return lax.broadcasted_iota(jnp.int32, shape, dim)


def frame_facts(me, len_ref):
    lens = len_ref[...].astype(F32)
    utts, devices = lens.shape
    lane = iota((devices, devices), 1)
    sub = iota((devices, devices), 0)
    owner_len = jnp.sum(lens, axis=0, keepdims=True)
    lane_row = iota((1, devices), 1)
    own_low = jnp.sum(jnp.where(lane_row < me, owner_len, 0.0), axis=1, keepdims=True)
    own_high = own_low + jnp.sum(jnp.where(lane_row == me, owner_len, 0.0), axis=1, keepdims=True)
    start = jnp.sum(jnp.where(lane < sub, owner_len, 0.0), axis=1, keepdims=True)
    total = (devices * SHARD) * 1.0
    frame = (iota((1, WIN), 1) + (me * SHARD - CTX)).astype(F32)
    begin = jnp.zeros((1, WIN), F32)
    end = jnp.full((1, WIN), total, F32)
    for u in range(utts):
        reached = start <= frame
        begin = jnp.maximum(begin, jnp.max(jnp.where(reached, start, 0.0), axis=0, keepdims=True))
        end = jnp.minimum(end, jnp.min(jnp.where(reached, total, start), axis=0, keepdims=True))
        start = start + jnp.sum(
            jnp.where(lane == sub, lens[u : u + 1, :], 0.0), axis=1, keepdims=True
        )
    return frame, begin, end, own_low, own_high


def window_taps(frame, begin, own_low, own_high, own_ref, up_ref, down_ref, x_ref):
    low = frame[:, 128:512] >= own_low
    high = frame[:, 640:] < own_high
    win = jnp.concatenate(
        [
            up_ref[:, :128].astype(F32),
            jnp.where(low, own_ref[:, :384].astype(F32), up_ref[:, 128:].astype(F32)),
            own_ref[:, 384:512].astype(F32),
            jnp.where(high, own_ref[:, 512:768].astype(F32), down_ref[...].astype(F32)),
        ],
        axis=1,
    )
    prev = pltpu.roll(win[MEL:], 1, 1)
    fresh = begin == frame
    row = iota((16, WIN), 0)
    ones = jnp.where(row < 3, 1.0, 0.0)
    first = jnp.where((row == 3) & fresh, 1.0, ones)
    head = jnp.where(fresh, 0.0, prev[2 * MEL :])
    x_ref[0] = jnp.concatenate([prev, first], axis=0).T.astype(BF16)
    x_ref[1] = jnp.concatenate([head, win[: 2 * MEL], ones], axis=0).T.astype(BF16)
    x_ref[2] = jnp.concatenate([win[MEL:], ones], axis=0).T.astype(BF16)


def second_weights(k2_ref, w2_ref):
    for tap in range(3):
        base = tap * 3 * CH
        w2_ref[tap, :, :CH] = k2_ref[base + CH : base + 3 * CH, :]
        w2_ref[tap, :CH, CH:] = jnp.zeros((CH, CH), BF16)
        w2_ref[tap, CH:, CH:] = k2_ref[base : base + CH, :]


def first_weights(pair, k1, bias_rows):
    row = iota((3 * MEL, CH), 0)
    frame_row = [(row >= MEL * a) & (row < MEL * (a + 1)) for a in range(3)]
    bin_row = row - jnp.where(row >= 2 * MEL, 2 * MEL, jnp.where(row >= MEL, MEL, 0))
    taps = []
    for b in range(3):
        taps.append(
            jnp.where(
                frame_row[0],
                k1[b : b + 1],
                jnp.where(frame_row[1], k1[3 + b : 4 + b], k1[6 + b : 7 + b]),
            )
        )
    halves = []
    for half in range(2):
        at = bin_row - (2 * (2 * pair + half) - 1)
        value = jnp.where(at == 0, taps[0], jnp.where(at == 1, taps[1], 0.0))
        value = jnp.where(at == 2, taps[2], value)
        halves.append(jnp.concatenate([value, bias_rows], axis=0))
    return jnp.concatenate(halves, axis=1).astype(BF16)


def layer_kernel(
    me_ref, len_ref, own_ref, up_ref, down_ref, k1_ref, b1_ref, k2_ref, b2_ref, gain_ref,
    we_hbm, wh_hbm, wo_hbm, out_ref,
    we_ref, wh_ref, wo_ref, x_ref, w2_ref, sec_ref, low_ref, emb_ref, norm_ref,
    q_ref, k_ref, vt_ref, mask_ref, mixed_ref, sems,
):
    copies = [
        pltpu.make_async_copy(src, dst, sems.at[i])
        for i, (src, dst) in enumerate(((we_hbm, we_ref), (wh_hbm, wh_ref), (wo_hbm, wo_ref)))
    ]
    for copy in copies:
        copy.start()
    frame, begin, end, own_low, own_high = frame_facts(me_ref[0], len_ref)
    window_taps(frame, begin, own_low, own_high, own_ref, up_ref, down_ref, x_ref)
    second_weights(k2_ref, w2_ref)
    low_ref[...] = jnp.zeros_like(low_ref)
    bias = b1_ref[...]
    b_high = bias.astype(BF16).astype(F32)
    b_mid = (bias - b_high).astype(BF16).astype(F32)
    b_low = bias - b_high - b_mid
    row = iota((16, CH), 0)
    bias_rows = jnp.where(row == 0, b_high, jnp.where(row == 1, b_mid, b_low))
    bias_rows = jnp.where(row < 3, bias_rows, jnp.where(row == 3, -1e30, 0.0))
    k1 = k1_ref[...].astype(F32)
    bias_2 = b2_ref[...]

    def conv_pair(pair, carry):
        w1 = first_weights(pair, k1, bias_rows)
        for t in range(WIN // ROWS):
            rows = slice(t * ROWS, (t + 1) * ROWS)
            acc = None
            for tap in range(3):
                h = jnp.dot(x_ref[tap, rows, :], w1, preferred_element_type=F32)
                h = jnp.maximum(h, 0.0).astype(BF16)
                part = jnp.dot(h, w2_ref[tap], preferred_element_type=F32)
                acc = part if acc is None else acc + part
            value = jnp.maximum(acc[:, :CH] + low_ref[rows, :] + bias_2, 0.0).astype(BF16)
            low_ref[rows, :] = acc[:, CH:]
            sec_ref[rows, pl.ds(pl.multiple_of(pair * CH, CH), CH)] = value
        return carry

    lax.fori_loop(0, PAIRS, conv_pair, 0)

    copies[0].wait()
    gain = gain_ref[...]
    for t in range(WIN // ROWS):
        rows = slice(t * ROWS, (t + 1) * ROWS)
        emb = jnp.dot(sec_ref[rows, :], we_ref[...], preferred_element_type=F32).astype(BF16)
        emb_ref[rows, :] = emb
        values = emb.astype(F32)
        center = values - jnp.mean(values, axis=1, keepdims=True)
        spread = jnp.mean(center * center, axis=1, keepdims=True)
        norm_ref[rows, :] = (center * lax.rsqrt(spread + 1e-05) * gain).astype(BF16)

    copies[1].wait()
    q = jnp.dot(norm_ref[CTX : CTX + SHARD, :], wh_ref[:, :D], preferred_element_type=F32)
    q_ref[...] = q.astype(BF16) * (HEAD**-0.5)
    for t in range(WIN // ROWS):
        rows = slice(t * ROWS, (t + 1) * ROWS)
        k = jnp.dot(norm_ref[rows, :], wh_ref[:, D : 2 * D], preferred_element_type=F32)
        k_ref[rows, :] = k.astype(BF16)
    for t in range(WIN // 128):
        rows = slice(t * 128, (t + 1) * 128)
        v = jnp.dot(norm_ref[rows, :], wh_ref[:, 2 * D :], preferred_element_type=F32)
        vt_ref[:, rows] = v.T.astype(BF16)

    query = frame[:, CTX : CTX + SHARD]
    q_begin = begin[:, CTX : CTX + SHARD]
    span_at = jnp.floor((query - q_begin) * (1.0 / SPAN)) * SPAN
    key_low = q_begin + jnp.maximum(span_at - LEFT_SPANS * SPAN, 0.0)
    key_high = jnp.minimum(q_begin + span_at + SPAN, end[:, CTX : CTX + SHARD])
    first_frame = (me_ref[0] * SHARD - CTX).astype(F32)
    for i in range(SHARD // QROWS):
        cols = slice(i * QROWS, (i + 1) * QROWS)
        key = iota((KROWS, QROWS), 0).astype(F32) + (first_frame + i * QROWS)
        seen = (key >= key_low[:, cols]) & (key < key_high[:, cols])
        mask_ref[:, cols] = jnp.where(seen, 0.0, -jnp.inf)

    lane = iota((QROWS, 2 * HEAD), 1)

    def attend_tile(step, carry):
        i = step // (HEADS // 2)
        pair = step % (HEADS // 2)
        q_at = pl.multiple_of(i * QROWS, QROWS)
        col = pl.multiple_of(pair * 2 * HEAD, 2 * HEAD)
        keys = k_ref[pl.ds(q_at, KROWS), pl.ds(col, 2 * HEAD)]
        qs = q_ref[pl.ds(q_at, QROWS), pl.ds(col, 2 * HEAD)]
        zero = jnp.zeros_like(qs)
        both = jnp.concatenate(
            [jnp.where(lane < HEAD, qs, zero), jnp.where(lane >= HEAD, qs, zero)], axis=0
        )
        scores = lax.dot_general(keys, both, (((1,), (1,)), ((), ())), preferred_element_type=F32)
        mask = mask_ref[:, pl.ds(q_at, QROWS)]
        scores = scores + jnp.concatenate([mask, mask], axis=1)
        expd = jnp.exp(scores - jnp.max(scores, axis=0, keepdims=True))
        total = jnp.sum(expd, axis=0, keepdims=True)
        values = vt_ref[pl.ds(col, 2 * HEAD), pl.ds(q_at, KROWS)]
        mixed = jnp.dot(values, expd.astype(BF16), preferred_element_type=F32) / total
        mixed = jnp.concatenate([mixed[:HEAD, :QROWS], mixed[HEAD:, QROWS:]], axis=0)
        mixed_ref[pl.ds(q_at, QROWS), pl.ds(col, 2 * HEAD)] = mixed.T.astype(BF16)
        return carry

    lax.fori_loop(0, (SHARD // QROWS) * (HEADS // 2), attend_tile, 0)

    copies[2].wait()
    output = jnp.dot(mixed_ref[...], wo_ref[...], preferred_element_type=F32)
    output = output + emb_ref[CTX : CTX + SHARD, :].astype(F32)
    out_ref[...] = output.astype(BF16)


def layer(me, lens, own, up, down, k1, b1, k2, b2, gain, we, wh, wo, interpret=False):
    vmem = pl.BlockSpec(memory_space=pltpu.VMEM)
    any_spec = pl.BlockSpec(memory_space=pl.ANY)
    return pl.pallas_call(
        layer_kernel,
        out_shape=jax.ShapeDtypeStruct((SHARD, D), BF16),
        in_specs=[pl.BlockSpec(memory_space=pltpu.SMEM)] + [vmem] * 9 + [any_spec] * 3,
        out_specs=vmem,
        scratch_shapes=[
            pltpu.VMEM(we.shape, BF16),
            pltpu.VMEM(wh.shape, BF16),
            pltpu.VMEM(wo.shape, BF16),
            pltpu.VMEM((3, WIN, 256), BF16),
            pltpu.VMEM((3, 256, 256), BF16),
            pltpu.VMEM((WIN, PAIRS * CH), BF16),
            pltpu.VMEM((WIN, CH), F32),
            pltpu.VMEM((WIN, D), BF16),
            pltpu.VMEM((WIN, D), BF16),
            pltpu.VMEM((SHARD, D), BF16),
            pltpu.VMEM((WIN, D), BF16),
            pltpu.VMEM((D, WIN), BF16),
            pltpu.VMEM((KROWS, SHARD), F32),
            pltpu.VMEM((SHARD, D), BF16),
            pltpu.SemaphoreType.DMA((3,)),
        ],
        compiler_params=pltpu.CompilerParams(vmem_limit_bytes=56 * 1024 * 1024),
        interpret=interpret,
        name="layer",
    )(me, lens, own, up, down, k1, b1, k2, b2, gain, we, wh, wo)


def on_device(log_mel, lengths, k1, b1, k2, b2, we, gain, wh, wo):
    devices = lax.axis_size(AXES)
    me = lax.axis_index(AXES).astype(jnp.int32).reshape(1)
    own = log_mel.T
    ahead = [(i, i + 1) for i in range(devices - 1)]
    back = [(i + 1, i) for i in range(devices - 1)]
    up = lax.ppermute(own[:, CAP - SHARD :], AXES, ahead)
    down = lax.ppermute(own[:, : MARGIN + SPAN], AXES, back)
    return layer(
        me, lengths.T, own, up, down, k1, b1.reshape(1, -1), k2, b2.reshape(1, -1),
        gain.reshape(1, -1), we, wh, wo,
    )


def solution(mesh):
    return jax.shard_map(
        on_device,
        mesh=mesh,
        in_specs=(P(AXES, None), P(), P(), P(), P(), P(), P(), P(), P(), P()),
        out_specs=P(AXES, None),
        check_vma=False,
    )
```

```python
import jax
import jax.numpy as jnp
from jax import lax
from jax.experimental import pallas as pl
from jax.experimental.pallas import tpu as pltpu
from jax.sharding import PartitionSpec as P

HEADS = 16
SPAN = 64
LEFT_SPANS = 4
CTX = 320
SHARD = 512
MARGIN = 192
CAP = 896
WIN = CTX + SHARD + SPAN
MEL = 80
CH = 128
PAIRS = MEL // 4
D = 1024
HEAD = D // HEADS
ROWS = 448
QROWS = 128
KROWS = 512
AXES = ("seq", "inner")
F32 = jnp.float32
BF16 = jnp.bfloat16


def iota(shape, dim):
    return lax.broadcasted_iota(jnp.int32, shape, dim)


def frame_facts(me, len_ref):
    lens = len_ref[...].astype(F32)
    utts, devices = lens.shape
    lane = iota((devices, devices), 1)
    sub = iota((devices, devices), 0)
    owner_len = jnp.sum(lens, axis=0, keepdims=True)
    lane_row = iota((1, devices), 1)
    own_low = jnp.sum(jnp.where(lane_row < me, owner_len, 0.0), axis=1, keepdims=True)
    own_high = own_low + jnp.sum(jnp.where(lane_row == me, owner_len, 0.0), axis=1, keepdims=True)
    start = jnp.sum(jnp.where(lane < sub, owner_len, 0.0), axis=1, keepdims=True)
    total = (devices * SHARD) * 1.0
    frame = (iota((1, WIN), 1) + (me * SHARD - CTX)).astype(F32)
    begin = jnp.zeros((1, WIN), F32)
    end = jnp.full((1, WIN), total, F32)
    for u in range(utts):
        reached = start <= frame
        begin = jnp.maximum(begin, jnp.max(jnp.where(reached, start, 0.0), axis=0, keepdims=True))
        end = jnp.minimum(end, jnp.min(jnp.where(reached, total, start), axis=0, keepdims=True))
        start = start + jnp.sum(
            jnp.where(lane == sub, lens[u : u + 1, :], 0.0), axis=1, keepdims=True
        )
    return frame, begin, end, own_low, own_high


def window_taps(frame, begin, own_low, own_high, own_ref, up_ref, down_ref, x_ref):
    low = frame[:, 128:512] >= own_low
    high = frame[:, 640:] < own_high
    win = jnp.concatenate(
        [
            up_ref[:, :128].astype(F32),
            jnp.where(low, own_ref[:, :384].astype(F32), up_ref[:, 128:].astype(F32)),
            own_ref[:, 384:512].astype(F32),
            jnp.where(high, own_ref[:, 512:768].astype(F32), down_ref[...].astype(F32)),
        ],
        axis=1,
    )
    prev = pltpu.roll(win[MEL:], 1, 1)
    fresh = begin == frame
    row = iota((16, WIN), 0)
    ones = jnp.where(row < 3, 1.0, 0.0)
    first = jnp.where((row == 3) & fresh, 1.0, ones)
    head = jnp.where(fresh, 0.0, prev[2 * MEL :])
    x_ref[0] = jnp.concatenate([prev, first], axis=0).T.astype(BF16)
    x_ref[1] = jnp.concatenate([head, win[: 2 * MEL], ones], axis=0).T.astype(BF16)
    x_ref[2] = jnp.concatenate([win[MEL:], ones], axis=0).T.astype(BF16)


def second_weights(k2_ref, w2_ref):
    for tap in range(3):
        base = tap * 3 * CH
        row = tap * 2 * CH
        w2_ref[row : row + 2 * CH, :CH] = k2_ref[base + CH : base + 3 * CH, :]
        w2_ref[row : row + CH, CH:] = jnp.zeros((CH, CH), BF16)
        w2_ref[row + CH : row + 2 * CH, CH:] = k2_ref[base : base + CH, :]


def first_tiles(k1, odd):
    row = iota((8, CH), 0)
    tiles = []
    for at in (0,) if odd else (-1, 0):
        tile = []
        for tap in range(3):
            halves = []
            for half in range(2):
                low = (4 if odd else 0) + 2 * half - 1 - 8 * at
                value = jnp.zeros((8, CH), F32)
                for b in range(3):
                    value = jnp.where(row == low + b, k1[3 * tap + b : 3 * tap + b + 1], value)
                halves.append(value)
            tile.append(jnp.concatenate(halves, axis=1))
        tiles.append((at, tile))
    return tiles


def place_tiles(w1_ref, slot, step, tiles):
    first = 8 * (step + 1)
    for at, tile in tiles:
        for tap in range(3):
            w1_ref[slot, tap, pl.ds(pl.multiple_of(first + 8 * at, 8), 8), :] = tile[tap]
    clear = first + 8 * (tiles[0][0] - 1)
    for tap in range(3):
        w1_ref[slot, tap, pl.ds(pl.multiple_of(jnp.maximum(clear, 0), 8), 8), :] = jnp.zeros((8, 2 * CH), F32)


def layer_kernel(
    me_ref, len_ref, own_ref, up_ref, down_ref, k1_ref, b1_ref, k2_ref, b2_ref, gain_ref,
    we_hbm, wh_hbm, wo_hbm, out_ref,
    we_ref, wh_ref, wo_ref, x_ref, w1_ref, w2_ref, h_ref, sec_ref, low_ref, emb_ref, norm_ref,
    q_ref, k_ref, vt_ref, mask_ref, score_ref, peak_ref, prob_ref, mixed_ref, sems,
):
    copies = [
        pltpu.make_async_copy(src, dst, sems.at[i])
        for i, (src, dst) in enumerate(((we_hbm, we_ref), (wh_hbm, wh_ref), (wo_hbm, wo_ref)))
    ]
    for copy in copies:
        copy.start()
    frame, begin, end, own_low, own_high = frame_facts(me_ref[0], len_ref)
    window_taps(frame, begin, own_low, own_high, own_ref, up_ref, down_ref, x_ref)
    second_weights(k2_ref, w2_ref)
    low_ref[...] = jnp.zeros_like(low_ref)
    bias = b1_ref[...]
    b_high = bias.astype(BF16).astype(F32)
    b_mid = (bias - b_high).astype(BF16).astype(F32)
    b_low = bias - b_high - b_mid
    row = iota((16, CH), 0)
    bias_rows = jnp.where(row == 0, b_high, jnp.where(row == 1, b_mid, b_low))
    bias_rows = jnp.where(row < 3, bias_rows, jnp.where(row == 3, -1e30, 0.0))
    bias_rows = jnp.concatenate([bias_rows, bias_rows], axis=1)
    k1 = k1_ref[...].astype(F32)
    bias_2 = b2_ref[...]
    tiles = [first_tiles(k1, odd) for odd in range(2)]
    w1_ref[...] = jnp.zeros_like(w1_ref)
    chunks = [slice(t * ROWS, (t + 1) * ROWS) for t in range(WIN // ROWS)]

    def conv_first(slot, step, rows, w1):
        for tap in range(3):
            h = jnp.dot(x_ref[tap, rows, :], w1, preferred_element_type=F32)
            h_ref[slot, rows, tap * 2 * CH : (tap + 1) * 2 * CH] = jnp.maximum(h, 0.0).astype(BF16)

    def conv_second(slot, pair, rows):
        acc = jnp.dot(h_ref[slot, rows, :], w2_ref[...], preferred_element_type=F32)
        value = jnp.maximum(acc[:, :CH] + low_ref[rows, :] + bias_2, 0.0).astype(BF16)
        low_ref[rows, :] = acc[:, CH:]
        sec_ref[rows, pl.ds(pl.multiple_of(pair * CH, CH), CH)] = value

    def first_matrix(slot, step):
        place_tiles(w1_ref, slot, step, tiles[slot])
        taps = w1_ref[slot, :, 8 : 8 + MEL, :].reshape(3 * MEL, 2 * CH)
        return jnp.concatenate([taps, bias_rows], axis=0).astype(BF16)

    def conv_pairs(step, last):
        w1 = first_matrix(1, step)
        for rows in chunks:
            conv_first(1, step, rows, w1)
            conv_second(0, 2 * step, rows)
        if not last:
            w1 = first_matrix(0, step + 1)
        for rows in chunks:
            if not last:
                conv_first(0, step + 1, rows, w1)
            conv_second(1, 2 * step + 1, rows)

    w1 = first_matrix(0, 0)
    for rows in chunks:
        conv_first(0, 0, rows, w1)

    def conv_step(step, carry):
        conv_pairs(step, False)
        return carry

    lax.fori_loop(0, PAIRS // 2 - 1, conv_step, 0)
    conv_pairs(PAIRS // 2 - 1, True)

    copies[0].wait()
    gain = gain_ref[...]
    for t in range(WIN // ROWS):
        rows = slice(t * ROWS, (t + 1) * ROWS)
        emb = jnp.dot(sec_ref[rows, :], we_ref[...], preferred_element_type=F32).astype(BF16)
        emb_ref[rows, :] = emb
        values = emb.astype(F32)
        center = values - jnp.mean(values, axis=1, keepdims=True)
        spread = jnp.mean(center * center, axis=1, keepdims=True)
        norm_ref[rows, :] = (center * lax.rsqrt(spread + 1e-05) * gain).astype(BF16)

    copies[1].wait()
    q = jnp.dot(norm_ref[CTX : CTX + SHARD, :], wh_ref[:, :D], preferred_element_type=F32)
    q_ref[...] = q.astype(BF16) * (HEAD**-0.5)
    for t in range(WIN // ROWS):
        rows = slice(t * ROWS, (t + 1) * ROWS)
        k = jnp.dot(norm_ref[rows, :], wh_ref[:, D : 2 * D], preferred_element_type=F32)
        k_ref[rows, :] = k.astype(BF16)
    for t in range(WIN // 128):
        rows = slice(t * 128, (t + 1) * 128)
        v = jnp.dot(norm_ref[rows, :], wh_ref[:, 2 * D :], preferred_element_type=F32)
        vt_ref[:, rows] = v.T.astype(BF16)

    query = frame[:, CTX : CTX + SHARD]
    q_begin = begin[:, CTX : CTX + SHARD]
    span_at = jnp.floor((query - q_begin) * (1.0 / SPAN)) * SPAN
    key_low = q_begin + jnp.maximum(span_at - LEFT_SPANS * SPAN, 0.0)
    key_high = jnp.minimum(q_begin + span_at + SPAN, end[:, CTX : CTX + SHARD])
    first_frame = (me_ref[0] * SHARD - CTX).astype(F32)
    for i in range(SHARD // QROWS):
        cols = slice(i * QROWS, (i + 1) * QROWS)
        key = iota((KROWS, QROWS), 0).astype(F32) + (first_frame + i * QROWS)
        seen = (key >= key_low[:, cols]) & (key < key_high[:, cols])
        mask_ref[:, cols] = jnp.where(seen, 0.0, -jnp.inf)

    lane = iota((QROWS, 2 * HEAD), 1)
    pairs = HEADS // 2
    steps = (SHARD // QROWS) * pairs
    summing = jnp.ones((16, KROWS), BF16)

    def places(step):
        q_at = pl.multiple_of((step // pairs) * QROWS, QROWS)
        col = pl.multiple_of((step % pairs) * 2 * HEAD, 2 * HEAD)
        return q_at, col

    def score(slot, step):
        q_at, col = places(step)
        qs = q_ref[pl.ds(q_at, QROWS), pl.ds(col, 2 * HEAD)]
        zero = jnp.zeros_like(qs)
        both = jnp.concatenate(
            [jnp.where(lane < HEAD, qs, zero), jnp.where(lane >= HEAD, qs, zero)], axis=0
        )
        keys = k_ref[pl.ds(q_at, KROWS), pl.ds(col, 2 * HEAD)]
        scores = lax.dot_general(keys, both, (((1,), (1,)), ((), ())), preferred_element_type=F32)
        mask = mask_ref[:, pl.ds(q_at, QROWS)]
        scores = scores + jnp.concatenate([mask, mask], axis=1)
        score_ref[slot] = scores
        peak_ref[slot] = jnp.max(scores, axis=0, keepdims=True)

    def weigh(slot):
        prob_ref[slot] = jnp.exp(score_ref[slot] - peak_ref[slot]).astype(BF16)

    def mix(slot, step):
        q_at, col = places(step)
        values = vt_ref[pl.ds(col, 2 * HEAD), pl.ds(q_at, KROWS)]
        values = jnp.concatenate([values, summing], axis=0)
        mixed = jnp.dot(values, prob_ref[slot], preferred_element_type=F32)
        mixed = mixed[: 2 * HEAD] / mixed[2 * HEAD : 2 * HEAD + 1]
        mixed = jnp.concatenate([mixed[:HEAD, :QROWS], mixed[HEAD:, QROWS:]], axis=0)
        mixed_ref[pl.ds(q_at, QROWS), pl.ds(col, 2 * HEAD)] = mixed.T.astype(BF16)

    def attend_two(it, carry):
        for slot in range(2):
            mix(slot, 2 * it + slot)
        for slot in range(2):
            weigh(slot)
        for slot in range(2):
            score(slot, 2 * it + 4 + slot)
        return carry

    for slot in range(2):
        score(slot, slot)
    for slot in range(2):
        weigh(slot)
    for slot in range(2):
        score(slot, 2 + slot)
    lax.fori_loop(0, steps // 2 - 2, attend_two, 0)
    for slot in range(2):
        mix(slot, steps - 4 + slot)
    for slot in range(2):
        weigh(slot)
    for slot in range(2):
        mix(slot, steps - 2 + slot)

    copies[2].wait()
    output = jnp.dot(mixed_ref[...], wo_ref[...], preferred_element_type=F32)
    output = output + emb_ref[CTX : CTX + SHARD, :].astype(F32)
    out_ref[...] = output.astype(BF16)


def layer(me, lens, own, up, down, k1, b1, k2, b2, gain, we, wh, wo, interpret=False):
    vmem = pl.BlockSpec(memory_space=pltpu.VMEM)
    any_spec = pl.BlockSpec(memory_space=pl.ANY)
    return pl.pallas_call(
        layer_kernel,
        out_shape=jax.ShapeDtypeStruct((SHARD, D), BF16),
        in_specs=[pl.BlockSpec(memory_space=pltpu.SMEM)] + [vmem] * 9 + [any_spec] * 3,
        out_specs=vmem,
        scratch_shapes=[
            pltpu.VMEM(we.shape, BF16),
            pltpu.VMEM(wh.shape, BF16),
            pltpu.VMEM(wo.shape, BF16),
            pltpu.VMEM((3, WIN, 256), BF16),
            pltpu.VMEM((2, 3, MEL + 16, 2 * CH), F32),
            pltpu.VMEM((3 * 2 * CH, 2 * CH), BF16),
            pltpu.VMEM((2, WIN, 3 * 2 * CH), BF16),
            pltpu.VMEM((WIN, PAIRS * CH), BF16),
            pltpu.VMEM((WIN, CH), F32),
            pltpu.VMEM((WIN, D), BF16),
            pltpu.VMEM((WIN, D), BF16),
            pltpu.VMEM((SHARD, D), BF16),
            pltpu.VMEM((WIN, D), BF16),
            pltpu.VMEM((D, WIN), BF16),
            pltpu.VMEM((KROWS, SHARD), F32),
            pltpu.VMEM((2, KROWS, 2 * QROWS), F32),
            pltpu.VMEM((2, 1, 2 * QROWS), F32),
            pltpu.VMEM((2, KROWS, 2 * QROWS), BF16),
            pltpu.VMEM((SHARD, D), BF16),
            pltpu.SemaphoreType.DMA((3,)),
        ],
        compiler_params=pltpu.CompilerParams(vmem_limit_bytes=56 * 1024 * 1024),
        interpret=interpret,
        name="layer",
    )(me, lens, own, up, down, k1, b1, k2, b2, gain, we, wh, wo)


def on_device(log_mel, lengths, k1, b1, k2, b2, we, gain, wh, wo):
    devices = lax.axis_size(AXES)
    me = lax.axis_index(AXES).astype(jnp.int32).reshape(1)
    own = log_mel.T
    ahead = [(i, i + 1) for i in range(devices - 1)]
    back = [(i + 1, i) for i in range(devices - 1)]
    up = lax.ppermute(own[:, CAP - SHARD :], AXES, ahead)
    down = lax.ppermute(own[:, : MARGIN + SPAN], AXES, back)
    return layer(
        me, lengths.T, own, up, down, k1, b1.reshape(1, -1), k2, b2.reshape(1, -1),
        gain.reshape(1, -1), we, wh, wo,
    )


def solution(mesh):
    return jax.shard_map(
        on_device,
        mesh=mesh,
        in_specs=(P(AXES, None), P(), P(), P(), P(), P(), P(), P(), P(), P()),
        out_specs=P(AXES, None),
        check_vma=False,
    )
```

```python
import jax
import jax.numpy as jnp
from jax import lax
from jax.experimental import pallas as pl
from jax.experimental.pallas import tpu as pltpu
from jax.sharding import PartitionSpec as P

HEADS = 16
SPAN = 64
LEFT_SPANS = 4
CTX = 320
SHARD = 512
MARGIN = 192
CAP = 896
WIN = CTX + SHARD + SPAN
MEL = 80
CH = 128
PAIRS = MEL // 4
D = 1024
HEAD = D // HEADS
ROWS = 448
LEAD = 16
EARLY = 384
LATE = 256
QROWS = 128
KROWS = 512
AXES = ("seq", "inner")
F32 = jnp.float32
BF16 = jnp.bfloat16


def iota(shape, dim):
    return lax.broadcasted_iota(jnp.int32, shape, dim)


def frame_facts(me, len_ref, low, count):
    lens = len_ref[...].astype(F32)
    utts, devices = lens.shape
    lane = iota((devices, devices), 1)
    sub = iota((devices, devices), 0)
    owner_len = jnp.sum(lens, axis=0, keepdims=True)
    lane_row = iota((1, devices), 1)
    own_low = jnp.sum(jnp.where(lane_row < me, owner_len, 0.0), axis=1, keepdims=True)
    own_high = own_low + jnp.sum(jnp.where(lane_row == me, owner_len, 0.0), axis=1, keepdims=True)
    start = jnp.sum(jnp.where(lane < sub, owner_len, 0.0), axis=1, keepdims=True)
    total = (devices * SHARD) * 1.0
    frame = (iota((1, count), 1) + (me * SHARD - CTX + low)).astype(F32)
    begin = jnp.zeros((1, count), F32)
    end = jnp.full((1, count), total, F32)
    for u in range(utts):
        reached = start <= frame
        begin = jnp.maximum(begin, jnp.max(jnp.where(reached, start, 0.0), axis=0, keepdims=True))
        end = jnp.minimum(end, jnp.min(jnp.where(reached, total, start), axis=0, keepdims=True))
        start = start + jnp.sum(
            jnp.where(lane == sub, lens[u : u + 1, :], 0.0), axis=1, keepdims=True
        )
    return frame, begin, end, own_low, own_high


def frame_taps(raw, fresh, x_ref, joined_ref):
    count = raw.shape[1]
    ones = jnp.where(iota((16, count), 0) < 3, 1.0, 0.0)
    head = jnp.where(fresh, 0.0, pltpu.roll(raw[3 * MEL :], 1, 1))
    x_ref[0] = jnp.concatenate([head, raw[: 2 * MEL], ones], axis=0).T.astype(BF16)
    x_ref[1] = jnp.concatenate([raw[MEL:], ones], axis=0).T.astype(BF16)
    joined_ref[...] = jnp.broadcast_to(jnp.where(fresh, 0.0, 1.0), (CH, count)).T


def second_weights(k2_ref, w2_ref):
    for tap in range(3):
        base = tap * 3 * CH
        row = tap * 2 * CH
        w2_ref[row : row + 2 * CH, :CH] = k2_ref[base + CH : base + 3 * CH, :]
        w2_ref[row : row + CH, CH:] = jnp.zeros((CH, CH), BF16)
        w2_ref[row + CH : row + 2 * CH, CH:] = k2_ref[base : base + CH, :]


def first_tiles(k1, odd):
    row = iota((8, CH), 0)
    tiles = []
    for at in (0,) if odd else (-1, 0):
        tile = []
        for tap in range(3):
            halves = []
            for half in range(2):
                low = (4 if odd else 0) + 2 * half - 1 - 8 * at
                value = jnp.zeros((8, CH), F32)
                for b in range(3):
                    value = jnp.where(row == low + b, k1[3 * tap + b : 3 * tap + b + 1], value)
                halves.append(value)
            tile.append(jnp.concatenate(halves, axis=1))
        tiles.append((at, tile))
    return tiles


def place_tiles(w1_ref, slot, step, tiles):
    first = 8 * (step + 1)
    for at, tile in tiles:
        for tap in range(3):
            w1_ref[slot, tap, first + 8 * at : first + 8 * at + 8, :] = tile[tap]
    clear = first + 8 * (tiles[0][0] - 1)
    if clear >= 0:
        for tap in range(3):
            w1_ref[slot, tap, clear : clear + 8, :] = jnp.zeros((8, 2 * CH), F32)


def convolve(
    chunks, k1_ref, b1_ref, k2_ref, b2_ref, x_ref, joined_ref, w1_ref, w2_ref, h_ref, low_ref, sec_ref, done=None
):
    second_weights(k2_ref, w2_ref)
    low_ref[...] = jnp.zeros_like(low_ref)
    bias = b1_ref[...]
    b_high = bias.astype(BF16).astype(F32)
    b_mid = (bias - b_high).astype(BF16).astype(F32)
    b_low = bias - b_high - b_mid
    row = iota((16, CH), 0)
    bias_rows = jnp.where(row == 0, b_high, jnp.where(row == 1, b_mid, b_low))
    bias_rows = jnp.where(row < 3, bias_rows, 0.0)
    bias_rows = jnp.concatenate([bias_rows, bias_rows], axis=1)
    k1 = k1_ref[...].astype(F32)
    bias_2 = b2_ref[...]
    tiles = [first_tiles(k1, odd) for odd in range(2)]
    w1_ref[...] = jnp.zeros_like(w1_ref)

    def conv_first(slot, chunk, w1):
        at, lead, count, _ = chunk
        rows = slice(at, at + count)
        even = jnp.dot(x_ref[0, rows, :], w1, preferred_element_type=F32)
        h_ref[slot, rows, 2 * CH : 4 * CH] = jnp.maximum(even, 0.0).astype(BF16)
        odd = jnp.dot(x_ref[1, at - lead : at + count, :], w1, preferred_element_type=F32)
        odd = jnp.maximum(odd, 0.0)
        h_ref[slot, rows, 4 * CH :] = odd[lead:].astype(BF16)
        before = pltpu.roll(odd, 1, 0)[lead:]
        joined = joined_ref[rows, :]
        before = before * jnp.concatenate([joined, joined], axis=1)
        h_ref[slot, rows, : 2 * CH] = before.astype(BF16)

    def conv_second(slot, chunk, pair):
        at, _, count, to = chunk
        rows = slice(at, at + count)
        acc = jnp.dot(h_ref[slot, rows, :], w2_ref[...], preferred_element_type=F32)
        value = jnp.maximum(acc[:, :CH] + low_ref[rows, :] + bias_2, 0.0).astype(BF16)
        low_ref[rows, :] = acc[:, CH:]
        sec_ref[pl.ds(to, count), pair * CH : (pair + 1) * CH] = value

    def first_matrix(slot, step):
        place_tiles(w1_ref, slot, step, tiles[slot])
        taps = w1_ref[slot, :, 8 : 8 + MEL, :].reshape(3 * MEL, 2 * CH)
        return jnp.concatenate([taps, bias_rows], axis=0).astype(BF16)

    def conv_pairs(step, last):
        w1 = first_matrix(1, step)
        for chunk in chunks:
            conv_first(1, chunk, w1)
            conv_second(0, chunk, 2 * step)
        if not last:
            w1 = first_matrix(0, step + 1)
        for chunk in chunks:
            if not last:
                conv_first(0, chunk, w1)
            conv_second(1, chunk, 2 * step + 1)

    w1 = first_matrix(0, 0)
    for chunk in chunks:
        conv_first(0, chunk, w1)

    for step in range(PAIRS // 2):
        conv_pairs(step, step == PAIRS // 2 - 1)
        if done is not None:
            done(step)


def fetch(sources, targets, sems):
    copies = [
        pltpu.make_async_copy(src, dst, sems.at[i])
        for i, (src, dst) in enumerate(zip(sources, targets, strict=True))
    ]
    for copy in copies:
        copy.start()
    return copies


def early_rows(me):
    return jnp.where(lax.rem(me, 2) == 1, 256, 512)


def early_kernel(
    me_ref, chip_ref, len_hbm, own_hbm, k1_hbm, b1_hbm, k2_hbm, b2_hbm, out_hbm,
    len_ref, own_ref, k1_ref, b1_ref, k2_ref, b2_ref, sems,
    x_ref, joined_ref, w1_ref, w2_ref, h_ref, low_ref, sec_ref, out_sems,
):
    me = me_ref[0]
    first = early_rows(me) - 128
    copies = fetch(
        (len_hbm, own_hbm.at[:, pl.ds(pl.multiple_of(first - 128, 128), EARLY + 128)])
        + (k1_hbm, b1_hbm, k2_hbm, b2_hbm),
        (len_ref, own_ref, k1_ref, b1_ref, k2_ref, b2_ref),
        sems,
    )
    copies[0].wait()
    frame, begin, _, own_low, own_high = frame_facts(me, len_ref, first, EARLY + 128)
    chip = chip_ref[...].astype(F32)
    edge = jnp.where(lax.rem(me, 2) == 1, chip[:, 384:], chip[:, :128])
    other = jnp.concatenate([chip[:, 128:384], edge, chip[:, 128:256]], axis=1)
    owned = (frame >= own_low) & (frame < own_high)
    for copy in copies[1:]:
        copy.wait()
    raw = jnp.where(owned, own_ref[...].astype(F32), other)
    frame_taps(raw, begin == frame, x_ref, joined_ref)
    sent = []

    def send(step):
        cols = slice(step * 2 * CH, (step + 1) * 2 * CH)
        sent.append(pltpu.make_async_copy(sec_ref.at[:, cols], out_hbm.at[:, cols], out_sems.at[step]))
        sent[-1].start()

    convolve(
        [(128, LEAD, EARLY, 0)], k1_ref, b1_ref, k2_ref, b2_ref,
        x_ref, joined_ref, w1_ref, w2_ref, h_ref, low_ref, sec_ref, send,
    )
    for copy in sent:
        copy.wait()


def layer_kernel(
    me_ref, cross_ref, chip_ref, early_hbm, len_hbm, own_hbm, k1_hbm, b1_hbm, k2_hbm, b2_hbm, gain_hbm,
    we_hbm, wh_hbm, wo_hbm, out_hbm,
    len_ref, own_ref, k1_ref, b1_ref, k2_ref, b2_ref, gain_ref,
    we_ref, wh_ref, wo_ref, sems,
    x_ref, joined_ref, w1_ref, w2_ref, h_ref, low_ref, sec_ref, emb_ref, norm_ref,
    q_ref, k_ref, vt_ref, mask_ref, score_ref, peak_ref, prob_ref, mixed_ref, out_ref, out_sems,
):
    me = me_ref[0]
    odd = lax.rem(me, 2) == 1
    late = pl.multiple_of(jnp.where(odd, 640, 256), 128)
    late_own = pl.multiple_of(late - 256, 128)
    early = pl.multiple_of(early_rows(me), 128)
    copies = fetch(
        (len_hbm, own_hbm.at[:, :128], own_hbm.at[:, pl.ds(late_own, LATE + 128)])
        + (k1_hbm, b1_hbm, k2_hbm, b2_hbm, gain_hbm, we_hbm, early_hbm, wh_hbm, wo_hbm),
        (len_ref, own_ref.at[:, :128], own_ref.at[:, 128:])
        + (k1_ref, b1_ref, k2_ref, b2_ref, gain_ref, we_ref, sec_ref.at[pl.ds(early, EARLY), :], wh_ref, wo_ref),
        sems,
    )
    for copy in copies[:8]:
        copy.wait()
    copies = copies[8:]
    frame, begin, _, own_low, _ = frame_facts(me, len_ref, 0, 256)
    cross = cross_ref[...].astype(F32)
    up = jnp.where(odd, chip_ref[:, :256].astype(F32), cross[:, :256])
    raw = jnp.concatenate(
        [up[:, :128], jnp.where(frame[:, 128:] >= own_low, own_ref[:, :128].astype(F32), up[:, 128:])],
        axis=1,
    )
    late_frame, late_begin, _, own_low, own_high = frame_facts(me, len_ref, late - 128, LATE + 128)
    other = jnp.where(odd, jnp.concatenate([cross[:, :128], cross[:, :256]], axis=1), cross[:, 128:])
    owned = (late_frame >= own_low) & (late_frame < own_high)
    raw = jnp.concatenate([raw, jnp.where(owned, own_ref[:, 128:].astype(F32), other)], axis=1)
    fresh = jnp.concatenate([begin, late_begin], axis=1) == jnp.concatenate([frame, late_frame], axis=1)
    frame_taps(raw, fresh, x_ref, joined_ref)
    convolve(
        [(0, 0, 256, 0), (384, LEAD, LATE, late)], k1_ref, b1_ref, k2_ref, b2_ref,
        x_ref, joined_ref, w1_ref, w2_ref, h_ref, low_ref, sec_ref,
    )

    copies[0].wait()
    copies[1].wait()
    gain = gain_ref[...]
    for t in range(WIN // ROWS):
        rows = slice(t * ROWS, (t + 1) * ROWS)
        emb = jnp.dot(sec_ref[rows, :], we_ref[...], preferred_element_type=F32).astype(BF16)
        emb_ref[rows, :] = emb
        values = emb.astype(F32)
        center = values - jnp.mean(values, axis=1, keepdims=True)
        spread = jnp.mean(center * center, axis=1, keepdims=True)
        norm_ref[rows, :] = (center * lax.rsqrt(spread + 1e-05) * gain).astype(BF16)

    copies[2].wait()
    q = jnp.dot(norm_ref[CTX : CTX + SHARD, :], wh_ref[:, :D], preferred_element_type=F32)
    q_ref[...] = q.astype(BF16) * (HEAD**-0.5)
    for t in range(WIN // ROWS):
        rows = slice(t * ROWS, (t + 1) * ROWS)
        k = jnp.dot(norm_ref[rows, :], wh_ref[:, D : 2 * D], preferred_element_type=F32)
        k_ref[rows, :] = k.astype(BF16)
    for t in range(WIN // 128):
        rows = slice(t * 128, (t + 1) * 128)
        v = jnp.dot(norm_ref[rows, :], wh_ref[:, 2 * D :], preferred_element_type=F32)
        vt_ref[:, rows] = v.T.astype(BF16)

    query, q_begin, q_end, _, _ = frame_facts(me, len_ref, CTX, SHARD)
    span_at = jnp.floor((query - q_begin) * (1.0 / SPAN)) * SPAN
    key_low = q_begin + jnp.maximum(span_at - LEFT_SPANS * SPAN, 0.0)
    key_high = jnp.minimum(q_begin + span_at + SPAN, q_end)
    first_frame = (me_ref[0] * SHARD - CTX).astype(F32)
    for i in range(SHARD // QROWS):
        cols = slice(i * QROWS, (i + 1) * QROWS)
        key = iota((KROWS, QROWS), 0).astype(F32) + (first_frame + i * QROWS)
        seen = (key >= key_low[:, cols]) & (key < key_high[:, cols])
        mask_ref[:, cols] = jnp.where(seen, 0.0, -jnp.inf)

    lane = iota((QROWS, 2 * HEAD), 1)
    pairs = HEADS // 2
    steps = (SHARD // QROWS) * pairs
    summing = jnp.ones((16, KROWS), BF16)

    def places(step):
        q_at = (step // pairs) * QROWS
        col = (step % pairs) * 2 * HEAD
        return q_at, col

    def score(slot, step):
        q_at, col = places(step)
        qs = q_ref[pl.ds(q_at, QROWS), pl.ds(col, 2 * HEAD)]
        zero = jnp.zeros_like(qs)
        both = jnp.concatenate(
            [jnp.where(lane < HEAD, qs, zero), jnp.where(lane >= HEAD, qs, zero)], axis=0
        )
        keys = k_ref[pl.ds(q_at, KROWS), pl.ds(col, 2 * HEAD)]
        scores = lax.dot_general(keys, both, (((1,), (1,)), ((), ())), preferred_element_type=F32)
        mask = mask_ref[:, pl.ds(q_at, QROWS)]
        scores = scores + jnp.concatenate([mask, mask], axis=1)
        score_ref[slot] = scores
        peak_ref[slot] = jnp.max(scores, axis=0, keepdims=True)

    def weigh(slot):
        prob_ref[slot] = jnp.exp(score_ref[slot] - peak_ref[slot]).astype(BF16)

    def mix(slot, step):
        q_at, col = places(step)
        values = vt_ref[pl.ds(col, 2 * HEAD), pl.ds(q_at, KROWS)]
        values = jnp.concatenate([values, summing], axis=0)
        mixed = jnp.dot(values, prob_ref[slot], preferred_element_type=F32)
        mixed = mixed[: 2 * HEAD] / mixed[2 * HEAD : 2 * HEAD + 1]
        mixed = jnp.concatenate([mixed[:HEAD, :QROWS], mixed[HEAD:, QROWS:]], axis=0)
        mixed_ref[pl.ds(q_at, QROWS), pl.ds(col, 2 * HEAD)] = mixed.T.astype(BF16)

    def attend_two(it):
        for slot in range(2):
            mix(slot, 2 * it + slot)
        for slot in range(2):
            weigh(slot)
        for slot in range(2):
            score(slot, 2 * it + 4 + slot)

    for slot in range(2):
        score(slot, slot)
    for slot in range(2):
        weigh(slot)
    for slot in range(2):
        score(slot, 2 + slot)
    for it in range(steps // 2 - 2):
        attend_two(it)
    for slot in range(2):
        mix(slot, steps - 4 + slot)
    for slot in range(2):
        weigh(slot)
    for slot in range(2):
        mix(slot, steps - 2 + slot)

    copies[3].wait()
    sent = []
    for t in range(2):
        rows = slice(t * SHARD // 2, (t + 1) * SHARD // 2)
        output = jnp.dot(mixed_ref[rows, :], wo_ref[...], preferred_element_type=F32)
        residual = emb_ref[CTX + rows.start : CTX + rows.stop, :].astype(F32)
        out_ref[rows, :] = (output + residual).astype(BF16)
        sent.append(pltpu.make_async_copy(out_ref.at[rows, :], out_hbm.at[rows, :], out_sems.at[t]))
        sent[-1].start()
    for copy in sent:
        copy.wait()


VMEM = pl.BlockSpec(memory_space=pltpu.VMEM)
SMEM = pl.BlockSpec(memory_space=pltpu.SMEM)
HBM = pl.BlockSpec(memory_space=pltpu.HBM)
MIB = 1024 * 1024
EARLY_MIB = 63
LAYER_MIB = 63


def held(array, columns=None):
    shape = array.shape if columns is None else (array.shape[0], columns)
    return pltpu.VMEM(shape, array.dtype)


def conv_scratch(count):
    return [
        pltpu.VMEM((2, count, 256), BF16),
        pltpu.VMEM((count, CH), F32),
        pltpu.VMEM((2, 3, MEL + 16, 2 * CH), F32),
        pltpu.VMEM((3 * 2 * CH, 2 * CH), BF16),
        pltpu.VMEM((2, count, 3 * 2 * CH), BF16),
        pltpu.VMEM((count, CH), F32),
    ]


def early_frames(me, chip, lens, own, k1, b1, k2, b2):
    count = EARLY + 128
    return pl.pallas_call(
        early_kernel,
        out_shape=jax.ShapeDtypeStruct((EARLY, PAIRS * CH), BF16),
        in_specs=[SMEM, VMEM] + [HBM] * 6,
        out_specs=HBM,
        scratch_shapes=[held(lens), held(own, count), held(k1), held(b1), held(k2), held(b2)]
        + [pltpu.SemaphoreType.DMA((6,))]
        + conv_scratch(count)
        + [pltpu.VMEM((EARLY, PAIRS * CH), BF16), pltpu.SemaphoreType.DMA((PAIRS // 2,))],
        compiler_params=pltpu.CompilerParams(vmem_limit_bytes=int(EARLY_MIB * MIB)),
        cost_estimate=pl.CostEstimate(flops=10 * 10**9, bytes_accessed=3 * 10**6, transcendentals=0),
        name="early_frames",
    )(me, chip, lens, own, k1, b1, k2, b2)


def layer(me, cross, chip, early, lens, own, k1, b1, k2, b2, gain, we, wh, wo):
    return pl.pallas_call(
        layer_kernel,
        out_shape=jax.ShapeDtypeStruct((SHARD, D), BF16),
        in_specs=[SMEM] + [VMEM] * 2 + [HBM] * 11,
        out_specs=HBM,
        scratch_shapes=[held(lens), held(own, LATE + 256)]
        + [held(array) for array in (k1, b1, k2, b2, gain, we, wh, wo)]
        + [pltpu.SemaphoreType.DMA((12,))]
        + conv_scratch(LATE + 384)
        + [
            pltpu.VMEM((WIN, PAIRS * CH), BF16),
            pltpu.VMEM((WIN, D), BF16),
            pltpu.VMEM((WIN, D), BF16),
            pltpu.VMEM((SHARD, D), BF16),
            pltpu.VMEM((WIN, D), BF16),
            pltpu.VMEM((D, WIN), BF16),
            pltpu.VMEM((KROWS, SHARD), F32),
            pltpu.VMEM((2, KROWS, 2 * QROWS), F32),
            pltpu.VMEM((2, 1, 2 * QROWS), F32),
            pltpu.VMEM((2, KROWS, 2 * QROWS), BF16),
            pltpu.VMEM((SHARD, D), BF16),
            pltpu.VMEM((SHARD, D), BF16),
            pltpu.SemaphoreType.DMA((2,)),
        ],
        compiler_params=pltpu.CompilerParams(vmem_limit_bytes=int(LAYER_MIB * MIB)),
        cost_estimate=pl.CostEstimate(flops=40 * 10**9, bytes_accessed=20 * 10**6, transcendentals=0),
        name="layer",
    )(me, cross, chip, early, lens, own, k1, b1, k2, b2, gain, we, wh, wo)


def cut_kernel(me_ref, own_hbm, cross_ref, chip_ref, sems):
    at = lax.rem(me_ref[0], 2) * (CAP - SHARD)
    other = (CAP - SHARD) - at
    copies = fetch(
        [own_hbm.at[:, pl.ds(pl.multiple_of(x, 128), SHARD)] for x in (at, other)],
        (cross_ref, chip_ref),
        sems,
    )
    for copy in copies:
        copy.wait()


def cut(me, own):
    part = jax.ShapeDtypeStruct((own.shape[0], SHARD), BF16)
    return pl.pallas_call(
        cut_kernel,
        out_shape=(part, part),
        in_specs=[SMEM, HBM],
        out_specs=(VMEM, VMEM),
        scratch_shapes=[pltpu.SemaphoreType.DMA((2,))],
        compiler_params=pltpu.CompilerParams(vmem_limit_bytes=4 * MIB),
        name="cut",
    )(me, own)


def on_device(log_mel, lengths, k1, b1, k2, b2, we, gain, wh, wo):
    devices = lax.axis_size(AXES)
    me = lax.axis_index(AXES).astype(jnp.int32).reshape(1)
    own = log_mel.T
    cross, chip = cut(me, own)
    ahead = [(i, i + 1) for i in range(0, devices, 2)]
    chip = lax.ppermute(chip, AXES, ahead + [(j, i) for i, j in ahead])
    ahead = [(i, i + 1) for i in range(1, devices - 1, 2)]
    cross = lax.ppermute(cross, AXES, ahead + [(j, i) for i, j in ahead])
    lens, b1, b2, gain = lengths.T, b1.reshape(1, -1), b2.reshape(1, -1), gain.reshape(1, -1)
    early = early_frames(me, chip, lens, own, k1, b1, k2, b2)
    return layer(me, cross, chip, early, lens, own, k1, b1, k2, b2, gain, we, wh, wo)


def solution(mesh):
    return jax.shard_map(
        on_device,
        mesh=mesh,
        in_specs=(P(AXES, None), P(), P(), P(), P(), P(), P(), P(), P(), P()),
        out_specs=P(AXES, None),
        check_vma=False,
    )
```

```python
import jax
import jax.numpy as jnp
from jax import lax
from jax.experimental import pallas as pl
from jax.experimental.pallas import tpu as pltpu
from jax.sharding import PartitionSpec as P

HEADS = 16
SPAN = 64
LEFT_SPANS = 4
CTX = 320
SHARD = 512
MARGIN = 192
CAP = 896
WIN = CTX + SHARD + SPAN
MEL = 80
CH = 128
PAIRS = MEL // 4
D = 1024
HEAD = D // HEADS
ROWS = 448
LEAD = 16
EARLY = 384
LATE = 256
QROWS = 128
KROWS = 512
AXES = ("seq", "inner")
LOG2E = 1.4426950408889634
F32 = jnp.float32
BF16 = jnp.bfloat16


def iota(shape, dim):
    return lax.broadcasted_iota(jnp.int32, shape, dim)


def frame_facts(me, len_ref, low, count):
    lens = len_ref[...].astype(F32)
    utts, devices = lens.shape
    lane = iota((devices, devices), 1)
    sub = iota((devices, devices), 0)
    owner_len = jnp.sum(lens, axis=0, keepdims=True)
    lane_row = iota((1, devices), 1)
    own_low = jnp.sum(jnp.where(lane_row < me, owner_len, 0.0), axis=1, keepdims=True)
    own_high = own_low + jnp.sum(jnp.where(lane_row == me, owner_len, 0.0), axis=1, keepdims=True)
    start = jnp.sum(jnp.where(lane < sub, owner_len, 0.0), axis=1, keepdims=True)
    total = (devices * SHARD) * 1.0
    frame = (iota((1, count), 1) + (me * SHARD - CTX + low)).astype(F32)
    begin = jnp.zeros((1, count), F32)
    end = jnp.full((1, count), total, F32)
    for u in range(utts):
        reached = start <= frame
        begin = jnp.maximum(begin, jnp.max(jnp.where(reached, start, 0.0), axis=0, keepdims=True))
        end = jnp.minimum(end, jnp.min(jnp.where(reached, total, start), axis=0, keepdims=True))
        start = start + jnp.sum(
            jnp.where(lane == sub, lens[u : u + 1, :], 0.0), axis=1, keepdims=True
        )
    return frame, begin, end, own_low, own_high


def frame_taps(raw, fresh, x_ref, joined_ref):
    count = raw.shape[1]
    ones = jnp.where(iota((16, count), 0) < 3, 1.0, 0.0)
    head = jnp.where(fresh, 0.0, pltpu.roll(raw[3 * MEL :], 1, 1))
    x_ref[0] = jnp.concatenate([head, raw[: 2 * MEL], ones], axis=0).T.astype(BF16)
    x_ref[1] = jnp.concatenate([raw[MEL:], ones], axis=0).T.astype(BF16)
    joined_ref[...] = jnp.broadcast_to(jnp.where(fresh, 0.0, 1.0), (CH, count)).T


def second_weights(k2_ref, w2_ref):
    for tap in range(3):
        base = tap * 3 * CH
        row = tap * 2 * CH
        w2_ref[row : row + 2 * CH, :CH] = k2_ref[base + CH : base + 3 * CH, :]
        w2_ref[row : row + CH, CH:] = jnp.zeros((CH, CH), BF16)
        w2_ref[row + CH : row + 2 * CH, CH:] = k2_ref[base : base + CH, :]


def first_tiles(k1, odd):
    row = iota((8, CH), 0)
    tiles = []
    for at in (0,) if odd else (-1, 0):
        tile = []
        for tap in range(3):
            halves = []
            for half in range(2):
                low = (4 if odd else 0) + 2 * half - 1 - 8 * at
                value = jnp.zeros((8, CH), F32)
                for b in range(3):
                    value = jnp.where(row == low + b, k1[3 * tap + b : 3 * tap + b + 1], value)
                halves.append(value)
            tile.append(jnp.concatenate(halves, axis=1))
        tiles.append((at, tile))
    return tiles


def place_tiles(w1_ref, slot, step, tiles):
    first = 8 * (step + 1)
    for at, tile in tiles:
        for tap in range(3):
            w1_ref[slot, tap, first + 8 * at : first + 8 * at + 8, :] = tile[tap]
    clear = first + 8 * (tiles[0][0] - 1)
    if clear >= 0:
        for tap in range(3):
            w1_ref[slot, tap, clear : clear + 8, :] = jnp.zeros((8, 2 * CH), F32)


def convolve(
    chunks, k1_ref, b1_ref, k2_ref, b2_ref, x_ref, joined_ref, w1_ref, w2_ref, h_ref, low_ref, sec_ref, done=None
):
    second_weights(k2_ref, w2_ref)
    low_ref[...] = jnp.zeros_like(low_ref)
    bias = b1_ref[...]
    b_high = bias.astype(BF16).astype(F32)
    b_mid = (bias - b_high).astype(BF16).astype(F32)
    b_low = bias - b_high - b_mid
    row = iota((16, CH), 0)
    bias_rows = jnp.where(row == 0, b_high, jnp.where(row == 1, b_mid, b_low))
    bias_rows = jnp.where(row < 3, bias_rows, 0.0)
    bias_rows = jnp.concatenate([bias_rows, bias_rows], axis=1)
    k1 = k1_ref[...].astype(F32)
    bias_2 = b2_ref[...]
    tiles = [first_tiles(k1, odd) for odd in range(2)]
    w1_ref[...] = jnp.zeros_like(w1_ref)

    def conv_first(slot, chunk, w1):
        at, lead, count, _ = chunk
        rows = slice(at, at + count)
        even = jnp.dot(x_ref[0, rows, :], w1, preferred_element_type=F32)
        h_ref[slot, rows, 2 * CH : 4 * CH] = jnp.maximum(even, 0.0).astype(BF16)
        odd = jnp.dot(x_ref[1, at - lead : at + count, :], w1, preferred_element_type=F32)
        odd = jnp.maximum(odd, 0.0)
        h_ref[slot, rows, 4 * CH :] = odd[lead:].astype(BF16)
        before = pltpu.roll(odd, 1, 0)[lead:]
        joined = joined_ref[rows, :]
        before = before * jnp.concatenate([joined, joined], axis=1)
        h_ref[slot, rows, : 2 * CH] = before.astype(BF16)

    def conv_second(slot, chunk, pair):
        at, _, count, to = chunk
        rows = slice(at, at + count)
        acc = jnp.dot(h_ref[slot, rows, :], w2_ref[...], preferred_element_type=F32)
        value = jnp.maximum(acc[:, :CH] + low_ref[rows, :] + bias_2, 0.0).astype(BF16)
        low_ref[rows, :] = acc[:, CH:]
        sec_ref[pl.ds(to, count), pair * CH : (pair + 1) * CH] = value

    def first_matrix(slot, step):
        place_tiles(w1_ref, slot, step, tiles[slot])
        taps = w1_ref[slot, :, 8 : 8 + MEL, :].reshape(3 * MEL, 2 * CH)
        return jnp.concatenate([taps, bias_rows], axis=0).astype(BF16)

    def conv_pairs(step, last):
        w1 = first_matrix(1, step)
        for chunk in chunks:
            conv_first(1, chunk, w1)
            conv_second(0, chunk, 2 * step)
        if not last:
            w1 = first_matrix(0, step + 1)
        for chunk in chunks:
            if not last:
                conv_first(0, chunk, w1)
            conv_second(1, chunk, 2 * step + 1)

    w1 = first_matrix(0, 0)
    for chunk in chunks:
        conv_first(0, chunk, w1)

    for step in range(PAIRS // 2):
        conv_pairs(step, step == PAIRS // 2 - 1)
        if done is not None:
            done(step)


def fetch(sources, targets, sems):
    copies = [
        pltpu.make_async_copy(src, dst, sems.at[i])
        for i, (src, dst) in enumerate(zip(sources, targets, strict=True))
    ]
    for copy in copies:
        copy.start()
    return copies


def early_rows(me):
    return jnp.where(lax.rem(me, 2) == 1, 256, 512)


def early_kernel(
    me_ref, chip_hbm, len_hbm, own_hbm, k1_hbm, b1_hbm, k2_hbm, b2_hbm, out_hbm,
    len_ref, own_ref, chip_ref, k1_ref, b1_ref, k2_ref, b2_ref, sems,
    x_ref, joined_ref, w1_ref, w2_ref, h_ref, low_ref, sec_ref, out_sems,
):
    me = me_ref[0]
    first = early_rows(me) - 128
    copies = fetch(
        (len_hbm, own_hbm.at[:, pl.ds(pl.multiple_of(first - 128, 128), EARLY + 128)])
        + (chip_hbm, k1_hbm, b1_hbm, k2_hbm, b2_hbm),
        (len_ref, own_ref, chip_ref, k1_ref, b1_ref, k2_ref, b2_ref),
        sems,
    )
    copies[0].wait()
    frame, begin, _, own_low, own_high = frame_facts(me, len_ref, first, EARLY + 128)
    for copy in copies[1:]:
        copy.wait()
    chip = chip_ref[...].astype(F32)
    edge = jnp.where(lax.rem(me, 2) == 1, chip[:, 384:], chip[:, :128])
    other = jnp.concatenate([chip[:, 128:384], edge, chip[:, 128:256]], axis=1)
    owned = (frame >= own_low) & (frame < own_high)
    raw = jnp.where(owned, own_ref[...].astype(F32), other)
    frame_taps(raw, begin == frame, x_ref, joined_ref)
    sent = []

    def send(step):
        cols = slice(step * 2 * CH, (step + 1) * 2 * CH)
        sent.append(pltpu.make_async_copy(sec_ref.at[:, cols], out_hbm.at[:, cols], out_sems.at[step]))
        sent[-1].start()

    convolve(
        [(128, LEAD, EARLY, 0)], k1_ref, b1_ref, k2_ref, b2_ref,
        x_ref, joined_ref, w1_ref, w2_ref, h_ref, low_ref, sec_ref, send,
    )
    for copy in sent:
        copy.wait()


def layer_kernel(
    me_ref, cross_hbm, chip_hbm, early_hbm, len_hbm, own_hbm, k1_hbm, b1_hbm, k2_hbm, b2_hbm, gain_hbm,
    we_hbm, wh_hbm, wo_hbm, out_hbm,
    len_ref, own_ref, chip_ref, cross_ref, k1_ref, b1_ref, k2_ref, b2_ref, gain_ref,
    we_ref, wh_ref, wo_ref, sems, weight_sems,
    x_ref, joined_ref, w1_ref, w2_ref, h_ref, low_ref, sec_ref, emb_ref, norm_ref,
    q_ref, k_ref, vt_ref, mask_ref, score_ref, peak_ref, prob_ref, mixed_ref, out_ref, out_sems,
):
    me = me_ref[0]
    odd = lax.rem(me, 2) == 1
    late = pl.multiple_of(jnp.where(odd, 640, 256), 128)
    late_own = pl.multiple_of(late - 256, 128)
    early = pl.multiple_of(early_rows(me), 128)
    copies = fetch(
        (len_hbm, own_hbm.at[:, :128], own_hbm.at[:, pl.ds(late_own, LATE + 128)], chip_hbm.at[:, :256])
        + (cross_hbm, k1_hbm, b1_hbm, k2_hbm, b2_hbm, gain_hbm),
        (len_ref, own_ref.at[:, :128], own_ref.at[:, 128:], chip_ref, cross_ref)
        + (k1_ref, b1_ref, k2_ref, b2_ref, gain_ref),
        sems,
    )
    copies[0].wait()
    frame, begin, _, own_low, _ = frame_facts(me, len_ref, 0, 256)
    late_frame, late_begin, _, own_low, own_high = frame_facts(me, len_ref, late - 128, LATE + 128)
    for copy in copies[1:]:
        copy.wait()
    copies = fetch(
        (we_hbm, early_hbm, wh_hbm, wo_hbm),
        (we_ref, sec_ref.at[pl.ds(early, EARLY), :], wh_ref, wo_ref),
        weight_sems,
    )
    cross = cross_ref[...].astype(F32)
    up = jnp.where(odd, chip_ref[...].astype(F32), cross[:, :256])
    raw = jnp.concatenate(
        [up[:, :128], jnp.where(frame[:, 128:] >= own_low, own_ref[:, :128].astype(F32), up[:, 128:])],
        axis=1,
    )
    other = jnp.where(odd, jnp.concatenate([cross[:, :128], cross[:, :256]], axis=1), cross[:, 128:])
    owned = (late_frame >= own_low) & (late_frame < own_high)
    raw = jnp.concatenate([raw, jnp.where(owned, own_ref[:, 128:].astype(F32), other)], axis=1)
    fresh = jnp.concatenate([begin, late_begin], axis=1) == jnp.concatenate([frame, late_frame], axis=1)
    frame_taps(raw, fresh, x_ref, joined_ref)
    convolve(
        [(0, 0, 256, 0), (384, LEAD, LATE, late)], k1_ref, b1_ref, k2_ref, b2_ref,
        x_ref, joined_ref, w1_ref, w2_ref, h_ref, low_ref, sec_ref,
    )

    copies[0].wait()
    copies[1].wait()
    gain = gain_ref[...]

    def embed(rows, cols):
        emb = jnp.dot(sec_ref[rows, :], we_ref[:, cols], preferred_element_type=F32)
        emb_ref[rows, cols] = emb.astype(BF16)

    def normalise(rows):
        values = emb_ref[rows, :].astype(F32)
        center = values - jnp.mean(values, axis=1, keepdims=True)
        spread = jnp.mean(center * center, axis=1, keepdims=True)
        norm_ref[rows, :] = (center * lax.rsqrt(spread + 1e-05) * gain).astype(BF16)

    def make_keys(rows, cols):
        k = jnp.dot(
            norm_ref[rows, :], wh_ref[:, D + cols.start : D + cols.stop], preferred_element_type=F32
        )
        k_ref[rows, cols] = k.astype(BF16)

    blocks = [slice(n * 256, (n + 1) * 256) for n in range(D // 256)]
    upper, lower = slice(0, ROWS), slice(ROWS, WIN)
    quarter = ROWS // len(blocks)
    for cols in blocks:
        embed(upper, cols)
    for n, cols in enumerate(blocks):
        embed(lower, cols)
        normalise(slice(n * quarter, (n + 1) * quarter))
    copies[2].wait()
    for n, cols in enumerate(blocks):
        make_keys(upper, cols)
        normalise(slice(ROWS + n * quarter, ROWS + (n + 1) * quarter))
    make_keys(lower, slice(0, D))
    q = jnp.dot(norm_ref[CTX : CTX + SHARD, :], wh_ref[:, :D], preferred_element_type=F32)
    q = q.astype(BF16).astype(F32) * (HEAD**-0.5 * LOG2E)
    q_high = q.astype(BF16)
    q_low = (q - q_high.astype(F32)).astype(BF16)
    for pair in range(HEADS // 2):
        cols = slice(pair * 2 * HEAD, (pair + 1) * 2 * HEAD)
        q_ref[:, pair * 4 * HEAD : pair * 4 * HEAD + 2 * HEAD] = q_high[:, cols]
        q_ref[:, pair * 4 * HEAD + 2 * HEAD : (pair + 1) * 4 * HEAD] = q_low[:, cols]
    for t in range(WIN // 128):
        rows = slice(t * 128, (t + 1) * 128)
        v = jnp.dot(norm_ref[rows, :], wh_ref[:, 2 * D :], preferred_element_type=F32)
        vt_ref[:, rows] = v.T.astype(BF16)

    query, q_begin, q_end, _, _ = frame_facts(me, len_ref, CTX, SHARD)
    span_at = jnp.floor((query - q_begin) * (1.0 / SPAN)) * SPAN
    key_low = q_begin + jnp.maximum(span_at - LEFT_SPANS * SPAN, 0.0)
    key_high = jnp.minimum(q_begin + span_at + SPAN, q_end)
    first_frame = (me_ref[0] * SHARD - CTX).astype(F32)
    for i in range(SHARD // QROWS):
        cols = slice(i * QROWS, (i + 1) * QROWS)
        key = iota((KROWS, QROWS), 0).astype(F32) + (first_frame + i * QROWS)
        seen = (key >= key_low[:, cols]) & (key < key_high[:, cols])
        mask_ref[:, cols] = jnp.where(seen, 0.0, -jnp.inf)

    lane = lax.rem(iota((QROWS, 4 * HEAD), 1), 2 * HEAD)
    pairs = HEADS // 2
    steps = (SHARD // QROWS) * pairs
    summing = jnp.ones((16, KROWS), BF16)

    def places(step):
        q_at = (step // pairs) * QROWS
        col = (step % pairs) * 2 * HEAD
        return q_at, col

    def score(slot, step):
        q_at, col = places(step)
        qs = q_ref[pl.ds(q_at, QROWS), pl.ds(2 * col, 4 * HEAD)]
        zero = jnp.zeros_like(qs)
        both = jnp.concatenate(
            [jnp.where(lane < HEAD, qs, zero), jnp.where(lane >= HEAD, qs, zero)], axis=0
        )
        keys = k_ref[pl.ds(q_at, KROWS), pl.ds(col, 2 * HEAD)]
        keys = jnp.concatenate([keys, keys], axis=1)
        scores = lax.dot_general(keys, both, (((1,), (1,)), ((), ())), preferred_element_type=F32)
        mask = mask_ref[:, pl.ds(q_at, QROWS)]
        scores = scores + jnp.concatenate([mask, mask], axis=1)
        score_ref[slot] = scores
        peak_ref[slot] = jnp.max(scores, axis=0, keepdims=True)

    def weigh(slot):
        prob_ref[slot] = jnp.exp2(score_ref[slot] - peak_ref[slot]).astype(BF16)

    def mix(slot, step):
        q_at, col = places(step)
        values = vt_ref[pl.ds(col, 2 * HEAD), pl.ds(q_at, KROWS)]
        values = jnp.concatenate([values, summing], axis=0)
        mixed = jnp.dot(values, prob_ref[slot], preferred_element_type=F32)
        mixed = mixed[: 2 * HEAD] / mixed[2 * HEAD : 2 * HEAD + 1]
        mixed = jnp.concatenate([mixed[:HEAD, :QROWS], mixed[HEAD:, QROWS:]], axis=0)
        mixed_ref[pl.ds(q_at, QROWS), pl.ds(col, 2 * HEAD)] = mixed.T.astype(BF16)

    def attend_two(it):
        for slot in range(2):
            mix(slot, 2 * it + slot)
        for slot in range(2):
            weigh(slot)
        for slot in range(2):
            score(slot, 2 * it + 4 + slot)

    for slot in range(2):
        score(slot, slot)
    for slot in range(2):
        weigh(slot)
    for slot in range(2):
        score(slot, 2 + slot)
    sent = []

    def project(rows, cols):
        output = jnp.dot(mixed_ref[rows, :], wo_ref[:, cols], preferred_element_type=F32)
        residual = emb_ref[CTX + rows.start : CTX + rows.stop, cols].astype(F32)
        out_ref[rows, cols] = (output + residual).astype(BF16)

    def send(rows):
        sent.append(pltpu.make_async_copy(out_ref.at[rows, :], out_hbm.at[rows, :], out_sems.at[len(sent)]))
        sent[-1].start()

    copies[3].wait()
    halves = slice(0, SHARD // 2), slice(SHARD // 2, SHARD)
    for it in range(steps // 2 - 2):
        attend_two(it)
        if steps // 4 <= it < steps // 4 + len(blocks):
            project(halves[0], blocks[it - steps // 4])
    send(halves[0])
    for slot in range(2):
        mix(slot, steps - 4 + slot)
    for slot in range(2):
        weigh(slot)
    for slot in range(2):
        mix(slot, steps - 2 + slot)
    project(halves[1], slice(0, D))
    send(halves[1])
    for copy in sent:
        copy.wait()


VMEM = pl.BlockSpec(memory_space=pltpu.VMEM)
SMEM = pl.BlockSpec(memory_space=pltpu.SMEM)
HBM = pl.BlockSpec(memory_space=pltpu.HBM)
MIB = 1024 * 1024
EARLY_MIB = 63
LAYER_MIB = 63


def held(array, columns=None):
    shape = array.shape if columns is None else (array.shape[0], columns)
    return pltpu.VMEM(shape, array.dtype)


def conv_scratch(count):
    return [
        pltpu.VMEM((2, count, 256), BF16),
        pltpu.VMEM((count, CH), F32),
        pltpu.VMEM((2, 3, MEL + 16, 2 * CH), F32),
        pltpu.VMEM((3 * 2 * CH, 2 * CH), BF16),
        pltpu.VMEM((2, count, 3 * 2 * CH), BF16),
        pltpu.VMEM((count, CH), F32),
    ]


def early_frames(me, chip, lens, own, k1, b1, k2, b2):
    count = EARLY + 128
    return pl.pallas_call(
        early_kernel,
        out_shape=jax.ShapeDtypeStruct((EARLY, PAIRS * CH), BF16),
        in_specs=[SMEM] + [HBM] * 7,
        out_specs=HBM,
        scratch_shapes=[held(lens), held(own, count), held(chip), held(k1), held(b1), held(k2), held(b2)]
        + [pltpu.SemaphoreType.DMA((7,))]
        + conv_scratch(count)
        + [pltpu.VMEM((EARLY, PAIRS * CH), BF16), pltpu.SemaphoreType.DMA((PAIRS // 2,))],
        compiler_params=pltpu.CompilerParams(vmem_limit_bytes=int(EARLY_MIB * MIB)),
        cost_estimate=pl.CostEstimate(flops=10 * 10**9, bytes_accessed=3 * 10**6, transcendentals=0),
        name="early_frames",
    )(me, chip, lens, own, k1, b1, k2, b2)


def layer(me, cross, chip, early, lens, own, k1, b1, k2, b2, gain, we, wh, wo):
    return pl.pallas_call(
        layer_kernel,
        out_shape=jax.ShapeDtypeStruct((SHARD, D), BF16),
        in_specs=[SMEM] + [HBM] * 13,
        out_specs=HBM,
        scratch_shapes=[held(lens), held(own, LATE + 256), held(chip, 256), held(cross)]
        + [held(array) for array in (k1, b1, k2, b2, gain, we, wh, wo)]
        + [pltpu.SemaphoreType.DMA((10,)), pltpu.SemaphoreType.DMA((4,))]
        + conv_scratch(LATE + 384)
        + [
            pltpu.VMEM((WIN, PAIRS * CH), BF16),
            pltpu.VMEM((WIN, D), BF16),
            pltpu.VMEM((WIN, D), BF16),
            pltpu.VMEM((SHARD, 2 * D), BF16),
            pltpu.VMEM((WIN, D), BF16),
            pltpu.VMEM((D, WIN), BF16),
            pltpu.VMEM((KROWS, SHARD), F32),
            pltpu.VMEM((2, KROWS, 2 * QROWS), F32),
            pltpu.VMEM((2, 1, 2 * QROWS), F32),
            pltpu.VMEM((2, KROWS, 2 * QROWS), BF16),
            pltpu.VMEM((SHARD, D), BF16),
            pltpu.VMEM((SHARD, D), BF16),
            pltpu.SemaphoreType.DMA((2,)),
        ],
        compiler_params=pltpu.CompilerParams(vmem_limit_bytes=int(LAYER_MIB * MIB)),
        cost_estimate=pl.CostEstimate(flops=40 * 10**9, bytes_accessed=20 * 10**6, transcendentals=0),
        name="layer",
    )(me, cross, chip, early, lens, own, k1, b1, k2, b2, gain, we, wh, wo)


def cut_kernel(me_ref, own_hbm, cross_ref, chip_ref, sems):
    at = lax.rem(me_ref[0], 2) * (CAP - SHARD)
    other = (CAP - SHARD) - at
    copies = fetch(
        [own_hbm.at[:, pl.ds(pl.multiple_of(x, 128), SHARD)] for x in (at, other)],
        (cross_ref, chip_ref),
        sems,
    )
    for copy in copies:
        copy.wait()


def cut(me, own):
    part = jax.ShapeDtypeStruct((own.shape[0], SHARD), BF16)
    return pl.pallas_call(
        cut_kernel,
        out_shape=(part, part),
        in_specs=[SMEM, HBM],
        out_specs=(VMEM, VMEM),
        scratch_shapes=[pltpu.SemaphoreType.DMA((2,))],
        compiler_params=pltpu.CompilerParams(vmem_limit_bytes=4 * MIB),
        name="cut",
    )(me, own)


def on_device(log_mel, lengths, k1, b1, k2, b2, we, gain, wh, wo):
    devices = lax.axis_size(AXES)
    me = lax.axis_index(AXES).astype(jnp.int32).reshape(1)
    own = log_mel.T
    cross, chip = cut(me, own)
    ahead = [(i, i + 1) for i in range(0, devices, 2)]
    chip = lax.ppermute(chip, AXES, ahead + [(j, i) for i, j in ahead])
    ahead = [(i, i + 1) for i in range(1, devices - 1, 2)]
    cross = lax.ppermute(cross, AXES, ahead + [(j, i) for i, j in ahead])
    lens, b1, b2, gain = lengths.T, b1.reshape(1, -1), b2.reshape(1, -1), gain.reshape(1, -1)
    early = early_frames(me, chip, lens, own, k1, b1, k2, b2)
    return layer(me, cross, chip, early, lens, own, k1, b1, k2, b2, gain, we, wh, wo)


def solution(mesh):
    return jax.shard_map(
        on_device,
        mesh=mesh,
        in_specs=(P(AXES, None), P(), P(), P(), P(), P(), P(), P(), P(), P()),
        out_specs=P(AXES, None),
        check_vma=False,
    )
```

```python
import jax
import jax.numpy as jnp
from jax import lax
from jax.experimental import pallas as pl
from jax.experimental.pallas import tpu as pltpu
from jax.sharding import PartitionSpec as P

HEADS = 16
SPAN = 64
LEFT_SPANS = 4
CTX = 320
SHARD = 512
MARGIN = 192
CAP = 896
WIN = CTX + SHARD + SPAN
MEL = 80
CH = 128
PAIRS = MEL // 4
D = 1024
HEAD = D // HEADS
ROWS = 448
LEAD = 16
EARLY = 384
LATE = 256
QROWS = 128
KROWS = 512
AXES = ("seq", "inner")
LOG2E = 1.4426950408889634
F32 = jnp.float32
BF16 = jnp.bfloat16


def iota(shape, dim):
    return lax.broadcasted_iota(jnp.int32, shape, dim)


def frame_facts(me, len_ref, low, count):
    lens = len_ref[...].astype(F32)
    utts, devices = lens.shape
    lane = iota((devices, devices), 1)
    sub = iota((devices, devices), 0)
    owner_len = jnp.sum(lens, axis=0, keepdims=True)
    lane_row = iota((1, devices), 1)
    own_low = jnp.sum(jnp.where(lane_row < me, owner_len, 0.0), axis=1, keepdims=True)
    own_high = own_low + jnp.sum(jnp.where(lane_row == me, owner_len, 0.0), axis=1, keepdims=True)
    start = jnp.sum(jnp.where(lane < sub, owner_len, 0.0), axis=1, keepdims=True)
    total = (devices * SHARD) * 1.0
    frame = (iota((1, count), 1) + (me * SHARD - CTX + low)).astype(F32)
    begin = jnp.zeros((1, count), F32)
    end = jnp.full((1, count), total, F32)
    for u in range(utts):
        reached = start <= frame
        begin = jnp.maximum(begin, jnp.max(jnp.where(reached, start, 0.0), axis=0, keepdims=True))
        end = jnp.minimum(end, jnp.min(jnp.where(reached, total, start), axis=0, keepdims=True))
        start = start + jnp.sum(
            jnp.where(lane == sub, lens[u : u + 1, :], 0.0), axis=1, keepdims=True
        )
    return frame, begin, end, own_low, own_high


def frame_taps(raw, fresh, x_ref, joined_ref):
    count = raw.shape[1]
    ones = jnp.where(iota((16, count), 0) < 3, 1.0, 0.0)
    head = jnp.where(fresh, 0.0, pltpu.roll(raw[3 * MEL :], 1, 1))
    x_ref[0] = jnp.concatenate([head, raw[: 2 * MEL], ones], axis=0).T.astype(BF16)
    x_ref[1] = jnp.concatenate([raw[MEL:], ones], axis=0).T.astype(BF16)
    joined_ref[...] = jnp.broadcast_to(jnp.where(fresh, 0.0, 1.0), (CH, count)).T


def second_weights(k2_ref, w2_ref):
    for tap in range(3):
        base = tap * 3 * CH
        row = tap * 2 * CH
        w2_ref[row : row + 2 * CH, :CH] = k2_ref[base + CH : base + 3 * CH, :]
        w2_ref[row : row + CH, CH:] = jnp.zeros((CH, CH), BF16)
        w2_ref[row + CH : row + 2 * CH, CH:] = k2_ref[base : base + CH, :]


def first_tiles(k1, odd):
    row = iota((8, CH), 0)
    tiles = []
    for at in (0,) if odd else (-1, 0):
        tile = []
        for tap in range(3):
            halves = []
            for half in range(2):
                low = (4 if odd else 0) + 2 * half - 1 - 8 * at
                value = jnp.zeros((8, CH), F32)
                for b in range(3):
                    value = jnp.where(row == low + b, k1[3 * tap + b : 3 * tap + b + 1], value)
                halves.append(value)
            tile.append(jnp.concatenate(halves, axis=1))
        tiles.append((at, tile))
    return tiles


def place_tiles(w1_ref, slot, step, tiles):
    first = 8 * (step + 1)
    for at, tile in tiles:
        for tap in range(3):
            w1_ref[slot, tap, first + 8 * at : first + 8 * at + 8, :] = tile[tap]
    clear = first + 8 * (tiles[0][0] - 1)
    if clear >= 0:
        for tap in range(3):
            w1_ref[slot, tap, clear : clear + 8, :] = jnp.zeros((8, 2 * CH), F32)


def convolve(
    chunks, k1_ref, b1_ref, k2_ref, b2_ref, x_ref, joined_ref, w1_ref, w2_ref, h_ref, low_ref, sec_ref, done=None
):
    second_weights(k2_ref, w2_ref)
    low_ref[...] = jnp.zeros_like(low_ref)
    bias = b1_ref[...]
    b_high = bias.astype(BF16).astype(F32)
    b_mid = (bias - b_high).astype(BF16).astype(F32)
    b_low = bias - b_high - b_mid
    row = iota((16, CH), 0)
    bias_rows = jnp.where(row == 0, b_high, jnp.where(row == 1, b_mid, b_low))
    bias_rows = jnp.where(row < 3, bias_rows, 0.0)
    bias_rows = jnp.concatenate([bias_rows, bias_rows], axis=1)
    k1 = k1_ref[...].astype(F32)
    bias_2 = b2_ref[...]
    tiles = [first_tiles(k1, odd) for odd in range(2)]
    w1_ref[...] = jnp.zeros_like(w1_ref)

    def conv_first(slot, chunk, w1):
        at, lead, count, _ = chunk
        rows = slice(at, at + count)
        even = jnp.dot(x_ref[0, rows, :], w1, preferred_element_type=F32)
        h_ref[slot, rows, 2 * CH : 4 * CH] = jnp.maximum(even, 0.0).astype(BF16)
        odd = jnp.dot(x_ref[1, at - lead : at + count, :], w1, preferred_element_type=F32)
        odd = jnp.maximum(odd, 0.0)
        h_ref[slot, rows, 4 * CH :] = odd[lead:].astype(BF16)
        before = pltpu.roll(odd, 1, 0)[lead:]
        joined = joined_ref[rows, :]
        before = before * jnp.concatenate([joined, joined], axis=1)
        h_ref[slot, rows, : 2 * CH] = before.astype(BF16)

    def conv_second(slot, chunk, pair):
        at, _, count, to = chunk
        rows = slice(at, at + count)
        acc = jnp.dot(h_ref[slot, rows, :], w2_ref[...], preferred_element_type=F32)
        value = jnp.maximum(acc[:, :CH] + low_ref[rows, :] + bias_2, 0.0).astype(BF16)
        low_ref[rows, :] = acc[:, CH:]
        sec_ref[pl.ds(to, count), pair * CH : (pair + 1) * CH] = value

    def first_matrix(slot, step):
        place_tiles(w1_ref, slot, step, tiles[slot])
        taps = w1_ref[slot, :, 8 : 8 + MEL, :].reshape(3 * MEL, 2 * CH)
        return jnp.concatenate([taps, bias_rows], axis=0).astype(BF16)

    def conv_pairs(step, last):
        w1 = first_matrix(1, step)
        for chunk in chunks:
            conv_first(1, chunk, w1)
            conv_second(0, chunk, 2 * step)
        if not last:
            w1 = first_matrix(0, step + 1)
        for chunk in chunks:
            if not last:
                conv_first(0, chunk, w1)
            conv_second(1, chunk, 2 * step + 1)

    w1 = first_matrix(0, 0)
    for chunk in chunks:
        conv_first(0, chunk, w1)

    for step in range(PAIRS // 2):
        conv_pairs(step, step == PAIRS // 2 - 1)
        if done is not None:
            done(step)


def fetch(sources, targets, sems):
    copies = [
        pltpu.make_async_copy(src, dst, sems.at[i])
        for i, (src, dst) in enumerate(zip(sources, targets, strict=True))
    ]
    for copy in copies:
        copy.start()
    return copies


def early_rows(me):
    return jnp.where(lax.rem(me, 2) == 1, 256, 512)


def early_kernel(
    me_ref, chip_hbm, len_hbm, own_hbm, k1_hbm, b1_hbm, k2_hbm, b2_hbm, out_hbm,
    len_ref, own_ref, chip_ref, k1_ref, b1_ref, k2_ref, b2_ref, sems,
    x_ref, joined_ref, w1_ref, w2_ref, h_ref, low_ref, sec_ref, out_sems,
):
    me = me_ref[0]
    first = early_rows(me) - 128
    copies = fetch(
        (len_hbm, own_hbm.at[:, pl.ds(pl.multiple_of(first - 128, 128), EARLY + 128)])
        + (chip_hbm, k1_hbm, b1_hbm, k2_hbm, b2_hbm),
        (len_ref, own_ref, chip_ref, k1_ref, b1_ref, k2_ref, b2_ref),
        sems,
    )
    copies[0].wait()
    frame, begin, _, own_low, own_high = frame_facts(me, len_ref, first, EARLY + 128)
    for copy in copies[1:]:
        copy.wait()
    chip = chip_ref[...].astype(F32)
    edge = jnp.where(lax.rem(me, 2) == 1, chip[:, 384:], chip[:, :128])
    other = jnp.concatenate([chip[:, 128:384], edge, chip[:, 128:256]], axis=1)
    owned = (frame >= own_low) & (frame < own_high)
    raw = jnp.where(owned, own_ref[...].astype(F32), other)
    frame_taps(raw, begin == frame, x_ref, joined_ref)
    sent = []

    def send(step):
        cols = slice(step * 2 * CH, (step + 1) * 2 * CH)
        sent.append(pltpu.make_async_copy(sec_ref.at[:, cols], out_hbm.at[:, cols], out_sems.at[step]))
        sent[-1].start()

    convolve(
        [(128, LEAD, EARLY, 0)], k1_ref, b1_ref, k2_ref, b2_ref,
        x_ref, joined_ref, w1_ref, w2_ref, h_ref, low_ref, sec_ref, send,
    )
    for copy in sent:
        copy.wait()


def layer_kernel(
    me_ref, cross_hbm, chip_hbm, early_hbm, len_hbm, own_hbm, k1_hbm, b1_hbm, k2_hbm, b2_hbm, gain_hbm,
    we_hbm, wh_hbm, wo_hbm, out_hbm,
    len_ref, own_ref, chip_ref, cross_ref, k1_ref, b1_ref, k2_ref, b2_ref, gain_ref,
    we_ref, wh_ref, wo_ref, sems, weight_sems,
    x_ref, joined_ref, w1_ref, w2_ref, h_ref, low_ref, sec_ref, emb_ref, norm_ref,
    q_ref, k_ref, vt_ref, mask_ref, score_ref, peak_ref, prob_ref, mixed_ref, out_ref, out_sems,
):
    me = me_ref[0]
    odd = lax.rem(me, 2) == 1
    late = pl.multiple_of(jnp.where(odd, 640, 256), 128)
    late_own = pl.multiple_of(late - 256, 128)
    early = pl.multiple_of(early_rows(me), 128)
    copies = fetch(
        (len_hbm, own_hbm.at[:, :128], own_hbm.at[:, pl.ds(late_own, LATE + 128)], chip_hbm.at[:, :256])
        + (cross_hbm, k1_hbm, b1_hbm, k2_hbm, b2_hbm, gain_hbm),
        (len_ref, own_ref.at[:, :128], own_ref.at[:, 128:], chip_ref, cross_ref)
        + (k1_ref, b1_ref, k2_ref, b2_ref, gain_ref),
        sems,
    )
    copies[0].wait()
    frame, begin, _, own_low, _ = frame_facts(me, len_ref, 0, 256)
    late_frame, late_begin, _, own_low, own_high = frame_facts(me, len_ref, late - 128, LATE + 128)
    for copy in copies[1:]:
        copy.wait()
    copies = fetch(
        (we_hbm, early_hbm, wh_hbm, wo_hbm),
        (we_ref, sec_ref.at[pl.ds(early, EARLY), :], wh_ref, wo_ref),
        weight_sems,
    )
    cross = cross_ref[...].astype(F32)
    up = jnp.where(odd, chip_ref[...].astype(F32), cross[:, :256])
    raw = jnp.concatenate(
        [up[:, :128], jnp.where(frame[:, 128:] >= own_low, own_ref[:, :128].astype(F32), up[:, 128:])],
        axis=1,
    )
    other = jnp.where(odd, jnp.concatenate([cross[:, :128], cross[:, :256]], axis=1), cross[:, 128:])
    owned = (late_frame >= own_low) & (late_frame < own_high)
    raw = jnp.concatenate([raw, jnp.where(owned, own_ref[:, 128:].astype(F32), other)], axis=1)
    fresh = jnp.concatenate([begin, late_begin], axis=1) == jnp.concatenate([frame, late_frame], axis=1)
    frame_taps(raw, fresh, x_ref, joined_ref)
    convolve(
        [(0, 0, 256, 0), (384, LEAD, LATE, late)], k1_ref, b1_ref, k2_ref, b2_ref,
        x_ref, joined_ref, w1_ref, w2_ref, h_ref, low_ref, sec_ref,
    )

    copies[0].wait()
    copies[1].wait()
    gain = gain_ref[...]

    def embed(rows, cols):
        emb = jnp.dot(sec_ref[rows, :], we_ref[:, cols], preferred_element_type=F32)
        emb_ref[rows, cols] = emb.astype(BF16)

    def normalise(rows):
        values = emb_ref[rows, :].astype(F32)
        center = values - jnp.mean(values, axis=1, keepdims=True)
        spread = jnp.mean(center * center, axis=1, keepdims=True)
        norm_ref[rows, :] = (center * lax.rsqrt(spread + 1e-05) * gain).astype(BF16)

    def make_keys(rows, cols):
        k = jnp.dot(
            norm_ref[rows, :], wh_ref[:, D + cols.start : D + cols.stop], preferred_element_type=F32
        )
        k_ref[rows, cols] = k.astype(BF16)

    blocks = [slice(n * 256, (n + 1) * 256) for n in range(D // 256)]
    upper, lower = slice(0, ROWS), slice(ROWS, WIN)
    quarter = ROWS // len(blocks)
    for cols in blocks:
        embed(upper, cols)
    for n, cols in enumerate(blocks):
        embed(lower, cols)
        normalise(slice(n * quarter, (n + 1) * quarter))
    copies[2].wait()
    for n, cols in enumerate(blocks):
        make_keys(upper, cols)
        normalise(slice(ROWS + n * quarter, ROWS + (n + 1) * quarter))
    make_keys(lower, slice(0, D))
    q = jnp.dot(norm_ref[CTX : CTX + SHARD, :], wh_ref[:, :D], preferred_element_type=F32)
    q = q.astype(BF16).astype(F32) * (HEAD**-0.5 * LOG2E)
    q_high = q.astype(BF16)
    q_low = (q - q_high.astype(F32)).astype(BF16)
    for pair in range(HEADS // 2):
        cols = slice(pair * 2 * HEAD, (pair + 1) * 2 * HEAD)
        q_ref[:, pair * 4 * HEAD : pair * 4 * HEAD + 2 * HEAD] = q_high[:, cols]
        q_ref[:, pair * 4 * HEAD + 2 * HEAD : (pair + 1) * 4 * HEAD] = q_low[:, cols]
    for t in range(WIN // 128):
        rows = slice(t * 128, (t + 1) * 128)
        v = jnp.dot(norm_ref[rows, :], wh_ref[:, 2 * D :], preferred_element_type=F32)
        vt_ref[:, rows] = v.T.astype(BF16)

    query, q_begin, q_end, _, _ = frame_facts(me, len_ref, CTX, SHARD)
    span_at = jnp.floor((query - q_begin) * (1.0 / SPAN)) * SPAN
    key_low = q_begin + jnp.maximum(span_at - LEFT_SPANS * SPAN, 0.0)
    key_high = jnp.minimum(q_begin + span_at + SPAN, q_end)
    first_frame = (me_ref[0] * SHARD - CTX).astype(F32)
    for i in range(SHARD // QROWS):
        cols = slice(i * QROWS, (i + 1) * QROWS)
        key = iota((KROWS, QROWS), 0).astype(F32) + (first_frame + i * QROWS)
        seen = (key >= key_low[:, cols]) & (key < key_high[:, cols])
        mask_ref[:, cols] = jnp.where(seen, 0.0, -jnp.inf)

    lane = lax.rem(iota((QROWS, 4 * HEAD), 1), 2 * HEAD)
    pairs = HEADS // 2
    steps = (SHARD // QROWS) * pairs
    summing = jnp.ones((16, KROWS), BF16)

    def places(step):
        q_at = (step // pairs) * QROWS
        col = (step % pairs) * 2 * HEAD
        return q_at, col

    def score(slot, step):
        q_at, col = places(step)
        qs = q_ref[pl.ds(q_at, QROWS), pl.ds(2 * col, 4 * HEAD)]
        zero = jnp.zeros_like(qs)
        both = jnp.concatenate(
            [jnp.where(lane < HEAD, qs, zero), jnp.where(lane >= HEAD, qs, zero)], axis=0
        )
        keys = k_ref[pl.ds(q_at, KROWS), pl.ds(col, 2 * HEAD)]
        keys = jnp.concatenate([keys, keys], axis=1)
        scores = lax.dot_general(keys, both, (((1,), (1,)), ((), ())), preferred_element_type=F32)
        mask = mask_ref[:, pl.ds(q_at, QROWS)]
        scores = scores + jnp.concatenate([mask, mask], axis=1)
        score_ref[slot] = scores
        peak_ref[slot] = jnp.max(scores, axis=0, keepdims=True)

    def weigh(slot):
        prob_ref[slot] = jnp.exp2(score_ref[slot] - peak_ref[slot]).astype(BF16)

    def mix(slot, step):
        q_at, col = places(step)
        values = vt_ref[pl.ds(col, 2 * HEAD), pl.ds(q_at, KROWS)]
        values = jnp.concatenate([values, summing], axis=0)
        mixed = jnp.dot(values, prob_ref[slot], preferred_element_type=F32)
        mixed = mixed[: 2 * HEAD] / mixed[2 * HEAD : 2 * HEAD + 1]
        mixed = jnp.concatenate([mixed[:HEAD, :QROWS], mixed[HEAD:, QROWS:]], axis=0)
        mixed_ref[pl.ds(q_at, QROWS), pl.ds(col, 2 * HEAD)] = mixed.T.astype(BF16)

    def attend_two(it):
        for slot in range(2):
            mix(slot, 2 * it + slot)
        for slot in range(2):
            weigh(slot)
        for slot in range(2):
            score(slot, 2 * it + 4 + slot)

    for slot in range(2):
        score(slot, slot)
    for slot in range(2):
        weigh(slot)
    for slot in range(2):
        score(slot, 2 + slot)
    sent = []

    def project(rows, cols):
        output = jnp.dot(mixed_ref[rows, :], wo_ref[:, cols], preferred_element_type=F32)
        residual = emb_ref[CTX + rows.start : CTX + rows.stop, cols].astype(F32)
        out_ref[rows, cols] = (output + residual).astype(BF16)

    def send(rows):
        sent.append(pltpu.make_async_copy(out_ref.at[rows, :], out_hbm.at[rows, :], out_sems.at[len(sent)]))
        sent[-1].start()

    copies[3].wait()
    halves = slice(0, SHARD // 2), slice(SHARD // 2, SHARD)
    for it in range(steps // 2 - 2):
        attend_two(it)
        if steps // 4 <= it < steps // 4 + len(blocks):
            project(halves[0], blocks[it - steps // 4])
    send(halves[0])
    for slot in range(2):
        mix(slot, steps - 4 + slot)
    for slot in range(2):
        weigh(slot)
    for slot in range(2):
        mix(slot, steps - 2 + slot)
    project(halves[1], slice(0, D))
    send(halves[1])
    for copy in sent:
        copy.wait()


VMEM = pl.BlockSpec(memory_space=pltpu.VMEM)
SMEM = pl.BlockSpec(memory_space=pltpu.SMEM)
HBM = pl.BlockSpec(memory_space=pltpu.HBM)
MIB = 1024 * 1024
EARLY_MIB = 58
LAYER_MIB = 63


def held(array, columns=None):
    shape = array.shape if columns is None else (array.shape[0], columns)
    return pltpu.VMEM(shape, array.dtype)


def conv_scratch(count):
    return [
        pltpu.VMEM((2, count, 256), BF16),
        pltpu.VMEM((count, CH), F32),
        pltpu.VMEM((2, 3, MEL + 16, 2 * CH), F32),
        pltpu.VMEM((3 * 2 * CH, 2 * CH), BF16),
        pltpu.VMEM((2, count, 3 * 2 * CH), BF16),
        pltpu.VMEM((count, CH), F32),
    ]


def early_frames(me, chip, lens, own, k1, b1, k2, b2):
    count = EARLY + 128
    return pl.pallas_call(
        early_kernel,
        out_shape=jax.ShapeDtypeStruct((EARLY, PAIRS * CH), BF16),
        in_specs=[SMEM] + [HBM] * 7,
        out_specs=HBM,
        scratch_shapes=[held(lens), held(own, count), held(chip), held(k1), held(b1), held(k2), held(b2)]
        + [pltpu.SemaphoreType.DMA((7,))]
        + conv_scratch(count)
        + [pltpu.VMEM((EARLY, PAIRS * CH), BF16), pltpu.SemaphoreType.DMA((PAIRS // 2,))],
        compiler_params=pltpu.CompilerParams(vmem_limit_bytes=int(EARLY_MIB * MIB)),
        cost_estimate=pl.CostEstimate(flops=10 * 10**9, bytes_accessed=3 * 10**6, transcendentals=0),
        name="early_frames",
    )(me, chip, lens, own, k1, b1, k2, b2)


def layer(me, cross, chip, early, lens, own, k1, b1, k2, b2, gain, we, wh, wo):
    return pl.pallas_call(
        layer_kernel,
        out_shape=jax.ShapeDtypeStruct((SHARD, D), BF16),
        in_specs=[SMEM] + [HBM] * 13,
        out_specs=HBM,
        scratch_shapes=[held(lens), held(own, LATE + 256), held(chip, 256), held(cross)]
        + [held(array) for array in (k1, b1, k2, b2, gain, we, wh, wo)]
        + [pltpu.SemaphoreType.DMA((10,)), pltpu.SemaphoreType.DMA((4,))]
        + conv_scratch(LATE + 384)
        + [
            pltpu.VMEM((WIN, PAIRS * CH), BF16),
            pltpu.VMEM((WIN, D), BF16),
            pltpu.VMEM((WIN, D), BF16),
            pltpu.VMEM((SHARD, 2 * D), BF16),
            pltpu.VMEM((WIN, D), BF16),
            pltpu.VMEM((D, WIN), BF16),
            pltpu.VMEM((KROWS, SHARD), F32),
            pltpu.VMEM((2, KROWS, 2 * QROWS), F32),
            pltpu.VMEM((2, 1, 2 * QROWS), F32),
            pltpu.VMEM((2, KROWS, 2 * QROWS), BF16),
            pltpu.VMEM((SHARD, D), BF16),
            pltpu.VMEM((SHARD, D), BF16),
            pltpu.SemaphoreType.DMA((2,)),
        ],
        compiler_params=pltpu.CompilerParams(vmem_limit_bytes=int(LAYER_MIB * MIB)),
        cost_estimate=pl.CostEstimate(flops=40 * 10**9, bytes_accessed=20 * 10**6, transcendentals=0),
        name="layer",
    )(me, cross, chip, early, lens, own, k1, b1, k2, b2, gain, we, wh, wo)


def cut_kernel(me_ref, own_hbm, cross_ref, chip_ref, sems):
    at = lax.rem(me_ref[0], 2) * (CAP - SHARD)
    other = (CAP - SHARD) - at
    copies = fetch(
        [own_hbm.at[:, pl.ds(pl.multiple_of(x, 128), SHARD)] for x in (at, other)],
        (cross_ref, chip_ref),
        sems,
    )
    for copy in copies:
        copy.wait()


def cut(me, own):
    part = jax.ShapeDtypeStruct((own.shape[0], SHARD), BF16)
    return pl.pallas_call(
        cut_kernel,
        out_shape=(part, part),
        in_specs=[SMEM, HBM],
        out_specs=(VMEM, VMEM),
        scratch_shapes=[pltpu.SemaphoreType.DMA((2,))],
        compiler_params=pltpu.CompilerParams(vmem_limit_bytes=4 * MIB),
        name="cut",
    )(me, own)


def on_device(log_mel, lengths, k1, b1, k2, b2, we, gain, wh, wo):
    devices = lax.axis_size(AXES)
    me = lax.axis_index(AXES).astype(jnp.int32).reshape(1)
    own = log_mel.T
    cross, chip = cut(me, own)
    ahead = [(i, i + 1) for i in range(0, devices, 2)]
    chip = lax.ppermute(chip, AXES, ahead + [(j, i) for i, j in ahead])
    ahead = [(i, i + 1) for i in range(1, devices - 1, 2)]
    cross = lax.ppermute(cross, AXES, ahead + [(j, i) for i, j in ahead])
    lens, b1, b2, gain = lengths.T, b1.reshape(1, -1), b2.reshape(1, -1), gain.reshape(1, -1)
    early = early_frames(me, chip, lens, own, k1, b1, k2, b2)
    return layer(me, cross, chip, early, lens, own, k1, b1, k2, b2, gain, we, wh, wo)


def solution(mesh):
    return jax.shard_map(
        on_device,
        mesh=mesh,
        in_specs=(P(AXES, None), P(), P(), P(), P(), P(), P(), P(), P(), P()),
        out_specs=P(AXES, None),
        check_vma=False,
    )
```
